1024 devices in a mesh: dp: 16 (over z), sp: 32 (over y, x), tp: 2 (over core).
Axes of the slice: x: 4, y: 8, z: 16, core: 2. Of those that a mesh axis runs over, the one named last changes fastest.
Arguments:
- qkv: bfloat16 [16, 64, 128, 1920], P('dp', None, ('sp', 'tp')), may hold values from -8 to 8
- out_grad: bfloat16 [16, 64, 128, 1280], P('dp', None, ('sp', 'tp')), may hold values from -16 to 16
- block_image: int32 [16, 64], P('dp'), may hold values from 0 to 47, never falling along the last dimension, each value on 1 to 2 neighbouring positions
- proj_weight: bfloat16 [640, 1280], replicated, may hold values from -0.25 to 0.25
- proj_bias: bfloat16 [1280], replicated, may hold values from -3 to 3
Outputs:
- branch_out: bfloat16 [16, 64, 128, 1280], P('dp', None, ('sp', 'tp'))
- qkv_grad: bfloat16 [16, 64, 128, 1920], P('dp', None, ('sp', 'tp'))
- weight_grad: float32 [640, 1280], P(None, ('sp', 'tp'))
- bias_grad: float32 [1280], P(('sp', 'tp'))
The draws below stay inside these ranges and needn't reach their ends.
Inputs may be any that keep to these rules, and one draw needn't show every extreme that they name: `block_image`: within a sample, ids never fall; every image covers 1 to 2 consecutive blocks and one covers exactly 2.
All inputs are finite; a program needn't handle non-finite values.
Results may differ from the reference program's by a relative error of at most 0.02.
Values may be sent and summed in bfloat16 or wider, within the bound.
No kernel may reach another device: no remote copies, remote signals or barrier semaphores. Data moves between devices by JAX's collectives and lax.ppermute only.
A program may use at most 128 MiB of HBM per device.

```python
import math
import jax
import jax.numpy as jnp
import numpy as np
from jax import lax

D = 1280
HEADS = 8
HD = 80
BLK = 128
IMGB = 2
SAMPLES = 16
BLOCKS = 64
ROWS = 131072


def draw_qkv(key, part):
    key = jax.random.fold_in(key, 7)
    full_shape = (SAMPLES, BLOCKS, BLK, 3 * HEADS * HD)
    key_base = jax.random.fold_in(key, 0)
    values = jnp.clip(1.3 * jax.random.normal(key_base, full_shape, jnp.float32), -7.5, 7.5)
    return values.astype(jnp.bfloat16)


def raised(entries, key, source, target, shards_of, factor):
    def block_of(dim):
        return (jnp.arange(entries.shape[dim]) // (entries.shape[dim] // shards_of)).reshape((-1,) + (1,) * (entries.ndim - 1 - dim))

    near = jax.random.permutation(key, shards_of)[block_of(target)]
    second = (block_of(target) + shards_of // 2) % shards_of
    return jnp.where((block_of(source) == near) | (block_of(source) == second), factor * entries, entries)


def steps_of(own_key, shape, cuts, least, largest):
    gain = 1.0
    for axis_at, shards_of in cuts:
        steps = jax.random.uniform(jax.random.fold_in(jax.random.fold_in(own_key, 6), axis_at), (shards_of,), jnp.float32, least / len(cuts), largest / len(cuts))
        gain = gain * jnp.repeat(jnp.exp(steps), shape[axis_at] // shards_of).reshape((-1,) + (1,) * (len(shape) - 1 - axis_at))
    return gain


def split_up(count, total, bound, lean):
    loads = [(1 << 20) // math.isqrt(rank ** lean) + 1 for rank in range(2, count + 1)]
    surplus, given = total - bound - (count - 1), [1] * (count - 1)
    while surplus > 0:
        candidates = [i for i in range(count - 1) if given[i] < bound]
        pool, remaining = sum([loads[i] for i in candidates]), surplus
        for i in candidates:
            more = min(bound - given[i], max(1, remaining * loads[i] // pool), surplus)
            given[i] = given[i] + more
            surplus = surplus - more
    return np.array([bound] + given)


def ragged_sizes(rng, amount, total, limit, lean):
    if amount == 2:
        one = jax.random.randint(rng, (), max(1, total - limit), min(limit, total - 1) + 1)
        return jnp.stack([one, total - one])
    sizes = jnp.asarray(split_up(amount, total, limit, lean), jnp.int32)
    couples = (amount - 1) // 2
    giver, sink = sizes[1:1 + 2 * couples:2], sizes[2:2 + 2 * couples:2]
    room = jnp.minimum(giver - 1, limit - sink)
    moved = jax.random.randint(jax.random.fold_in(rng, 1), (couples,), 0, 1 << 20) % (room + 1)
    sizes = sizes.at[1:1 + 2 * couples:2].set(giver - moved).at[2:2 + 2 * couples:2].set(sink + moved)
    return sizes[jax.random.permutation(jax.random.fold_in(rng, 2), amount)]


def gaussian(key, extent, spread, most, pieces=(), dtype=jnp.bfloat16):
    drawn = spread * jax.random.normal(key, extent, jnp.float32)
    if pieces:
        drawn = drawn * steps_of(key, extent, pieces, -0.22, 0.18)
    return jnp.clip(drawn, -most, most).astype(dtype)


def bell_draw_with(rng, shape, width, limit, cuts, heavy, dtype=jnp.bfloat16):
    values = width * jax.random.normal(rng, shape, jnp.float32)
    if cuts:
        values = values * steps_of(rng, shape, cuts, -0.22, 0.18)
    return jnp.clip(raised(values, jax.random.fold_in(rng, 3), *heavy), -limit, limit).astype(dtype)


def setup_inputs(seed: int = 0) -> dict:
    splits = jax.random.split(jax.random.key(seed), 6)
    qkv = draw_qkv(jax.random.fold_in(splits[5], 71), 0)
    out_grad = bell_draw_with(splits[1], (SAMPLES, BLOCKS, BLK, D), 1.0, 16.0, ((0, 16), (2, 64)), (2, 3, 64, 4.0))
    block_image = jax.vmap(lambda own: jnp.searchsorted(jnp.cumsum(ragged_sizes(own, (3 * BLOCKS) // 4, BLOCKS, IMGB, 0)), jnp.arange(BLOCKS), side="right"))(jax.random.split(splits[2], SAMPLES)).reshape((SAMPLES, BLOCKS)).astype(jnp.int32)
    proj_weight = gaussian(splits[3], (HEADS * HD, D), (HEADS * HD) ** -0.5, 0.25)
    proj_bias = gaussian(splits[4], (D,), 0.5, 3.0)
    return {"qkv": qkv, "out_grad": out_grad, "block_image": block_image, "proj_weight": proj_weight, "proj_bias": proj_bias}


masked_score = -1e30


def rounded(values):
    return lax.optimization_barrier(values.astype(jnp.bfloat16)).astype(jnp.float32)


def sample_pass(inputs, proj_weight, proj_bias):
    qkv_rows, grad_rows, images = inputs
    head_cols = HEADS * HD
    margin = IMGB - 1
    window_len = 2 * IMGB - 1
    score_scale = HD ** -0.5
    grad_flat = grad_rows.reshape(BLOCKS * BLK, D)
    out_delta = jnp.dot(grad_flat, proj_weight.T, preferred_element_type=jnp.float32).astype(jnp.bfloat16)
    split_qkv = qkv_rows.reshape(BLOCKS, BLK, 3, HEADS, HD).astype(jnp.float32)
    query_rows = split_qkv[:, :, 0]
    key_rows = split_qkv[:, :, 1]
    value_rows = split_qkv[:, :, 2]
    delta_rows = out_delta.reshape(BLOCKS, BLK, HEADS, HD).astype(jnp.float32)

    def window(field_rows):
        padded = jnp.pad(field_rows, ((margin, margin), (0, 0), (0, 0), (0, 0)))
        return jnp.concatenate([padded[offset:offset + BLOCKS] for offset in range(window_len)], axis=1)

    ids_padded = jnp.pad(images, (margin, margin), constant_values=-1)
    window_ids = jnp.stack([ids_padded[offset:offset + BLOCKS] for offset in range(window_len)], axis=1)
    key_ids = jnp.repeat(window_ids, BLK, axis=1)
    same_image = images[:, None, None, None] == key_ids[:, None, None, :]
    key_window = window(key_rows)
    value_window = window(value_rows)
    scores = jnp.einsum('bihd,bjhd->bhij', query_rows, key_window) * score_scale
    scores = jnp.where(same_image, scores, masked_score)
    row_max = jnp.max(scores, axis=-1, keepdims=True)
    exp_scores = jnp.exp(scores - row_max)
    probs_f = exp_scores / jnp.sum(exp_scores, axis=-1, keepdims=True)
    probs_bf = rounded(probs_f)
    attended = jnp.einsum('bhij,bjhd->bihd', probs_bf, value_window).astype(jnp.bfloat16)
    attended_rows = attended.reshape(BLOCKS * BLK, head_cols)
    branch = jnp.dot(attended_rows, proj_weight, preferred_element_type=jnp.float32) + proj_bias.astype(jnp.float32)
    branch = branch.astype(jnp.bfloat16).reshape(BLOCKS, BLK, D)
    prob_grad = jnp.einsum('bihd,bjhd->bhij', delta_rows, value_window)
    centre = jnp.sum(probs_f * prob_grad, axis=-1, keepdims=True)
    score_grad = rounded(probs_f * (prob_grad - centre) * score_scale)
    query_grad = jnp.einsum('bhij,bjhd->bihd', score_grad, key_window)
    key_grad_window = jnp.einsum('bhij,bihd->bjhd', score_grad, query_rows)
    value_grad_window = jnp.einsum('bhij,bihd->bjhd', probs_bf, delta_rows)

    def fold(window_grad):
        segments = window_grad.reshape(BLOCKS, window_len, BLK, HEADS, HD)
        folded = jnp.zeros((BLOCKS + 2 * margin, BLK, HEADS, HD), jnp.float32)
        for offset in range(window_len):
            folded = folded.at[offset:offset + BLOCKS].add(segments[:, offset])
        return folded[margin:margin + BLOCKS]

    stacked = jnp.stack([query_grad, fold(key_grad_window), fold(value_grad_window)], axis=2)
    qkv_grad = stacked.astype(jnp.bfloat16).reshape(BLOCKS, BLK, 3 * head_cols)
    weight_part = jnp.dot(attended_rows.T, grad_flat, preferred_element_type=jnp.float32)
    bias_part = jnp.sum(grad_flat.astype(jnp.float32), axis=0)
    return branch, qkv_grad, weight_part, bias_part


def reference(qkv, out_grad, block_image, proj_weight, proj_bias):
    branch, qkv_grad, weight_parts, bias_parts = lax.map(
        lambda inputs: sample_pass(inputs, proj_weight, proj_bias), (qkv, out_grad, block_image))
    grad_scale = ROWS ** -0.5
    weight_grad = jnp.sum(weight_parts, axis=0) * grad_scale
    bias_grad = jnp.sum(bias_parts, axis=0) * grad_scale
    return branch, qkv_grad, weight_grad, bias_grad
```

```python
import jax
import jax.numpy as jnp
import numpy as np
from jax import lax
from jax.experimental import pallas as pl
from jax.experimental.pallas import tpu as pltpu
from jax.sharding import PartitionSpec as P

HD = 80
BF = jnp.bfloat16
F32 = jnp.float32
masked_score = -1e30

VM = pl.BlockSpec(memory_space=pltpu.VMEM)
SM = pl.BlockSpec(memory_space=pltpu.SMEM)
PARAMS = pltpu.CompilerParams(vmem_limit_bytes=48 * 1024 * 1024)


def dot(a, b, ca=1, cb=0):
    return lax.dot_general(a, b, (((ca,), (cb,)), ((), ())), preferred_element_type=F32)


def call(kernel, outs, specs, *args):
    return pl.pallas_call(
        kernel,
        out_shape=outs,
        in_specs=specs,
        out_specs=jax.tree.map(lambda _: VM, outs),
        compiler_params=PARAMS,
    )(*args)


def arr(shape, dtype):
    return jax.ShapeDtypeStruct(shape, dtype)


def rows_at(row_of, count):
    n = row_of.shape[1]
    return jnp.where(lax.broadcasted_iota(jnp.int32, (count, n), 0) == row_of, 1.0, 0.0).astype(BF)


def slot_rows(shape, dim):
    i = lax.broadcasted_iota(jnp.int32, shape, dim)
    return ((i >> 2) & 3) * 256 + ((i >> 1) & 1) * 128 + (i >> 4) * 2 + (i & 1)


def send_kernel(qkv_ref, grad_ref, weight_ref, dst_ref, pick_ref, out_ref):
    grad = grad_ref[...]
    delta = dot(grad, weight_ref[...], 1, 1).astype(BF)
    pick = rows_at(pick_ref[...], 640)
    low = dot(grad[:, :640], pick).astype(BF)
    high = dot(grad[:, 640:], pick).astype(BF)
    blocks = []
    for t in range(2):
        picked = jnp.concatenate([low[:, t * 384:(t + 1) * 384], high[:, t * 384:(t + 1) * 384]], axis=1)
        for g in range(4):
            if g < 3:
                at = g * 640 + t * 320
                kind = qkv_ref[:, at:at + 320]
            else:
                kind = delta[:, t * 320:(t + 1) * 320]
            blocks.append(jnp.concatenate([kind, picked[:, g * 192:(g + 1) * 192]], axis=1))
    stack = jnp.concatenate(blocks, axis=0)
    out_ref[...] = dot(rows_at(dst_ref[...], 1024), stack).astype(BF)


def head_masks(rows):
    lane = lax.broadcasted_iota(jnp.int32, (rows, 320), 1)
    return [(lane >= h * HD) & (lane < (h + 1) * HD) for h in range(4)]


def by_head(x, masks):
    zero = jnp.zeros_like(x)
    return jnp.concatenate([jnp.where(m, x, zero) for m in masks], axis=0)


def own_head(x, masks):
    total = jnp.zeros((256, 320), F32)
    for h, m in enumerate(masks):
        total = jnp.where(m, x[h * 256:(h + 1) * 256], total)
    return total


def attend_kernel(double_ref, got_ref, att_ref, probs_ref, sorted_ref):
    sel = rows_at(slot_rows((1, 1024), 1), 1024)
    rows = dot(sel, got_ref[...]).astype(BF)
    sorted_ref[...] = rows
    query, key, value = rows[:256, :320], rows[256:512, :320], rows[512:768, :320]
    masks = head_masks(256)
    scores = dot(by_head(query, masks), key, 1, 1) * (HD ** -0.5)
    row = lax.broadcasted_iota(jnp.int32, (1024, 256), 0)
    col = lax.broadcasted_iota(jnp.int32, (1024, 256), 1)
    apart = (((row ^ col) >> 7) & 1) > double_ref[0]
    scores = jnp.where(apart, masked_score, scores)
    exp_scores = jnp.exp(scores - jnp.max(scores, axis=-1, keepdims=True))
    probs = exp_scores / jnp.sum(exp_scores, axis=-1, keepdims=True)
    probs_ref[...] = probs
    att_ref[...] = own_head(dot(probs.astype(BF), value), masks).astype(BF)


def back_kernel(sorted_ref, probs_ref, att_ref, out_ref):
    rows = sorted_ref[...]
    query, key = rows[:256, :320], rows[256:512, :320]
    value, delta = rows[512:768, :320], rows[768:, :320]
    masks = head_masks(256)
    query_heads, delta_heads = by_head(query, masks), by_head(delta, masks)
    probs = probs_ref[...]
    prob_grad = dot(delta_heads, value, 1, 1)
    centre = jnp.sum(probs * prob_grad, axis=-1, keepdims=True)
    score_grad = (probs * (prob_grad - centre) * (HD ** -0.5)).astype(BF)
    query_grad = own_head(dot(score_grad, key), masks).astype(BF)
    key_grad = dot(score_grad, query_heads, 0, 0).astype(BF)
    value_grad = dot(probs.astype(BF), delta_heads, 0, 0).astype(BF)
    stack = jnp.concatenate([att_ref[...], query_grad, key_grad, value_grad], axis=0)
    lane = lax.broadcasted_iota(jnp.int32, (1024, 1024), 1)
    back = jnp.where(lane == slot_rows((1024, 1), 0), 1.0, 0.0).astype(BF)
    out_ref[...] = dot(back, stack).astype(BF)


def weight_kernel(core_ref, sorted_ref, own_ref, other_ref, out_ref):
    rows = sorted_ref[...]
    grad = jnp.concatenate([rows[g * 256:(g + 1) * 256, 320:] for g in range(4)], axis=1)
    first = core_ref[0] == 0
    own, other = own_ref[...], other_ref[...]
    att = jnp.concatenate([jnp.where(first, own, other), jnp.where(first, other, own)], axis=1)
    part = dot(grad, att, 0, 0)
    sums = dot(jnp.ones((8, 256), BF), grad)[:1]
    row = lax.broadcasted_iota(jnp.int32, (768, 768), 0)
    col = lax.broadcasted_iota(jnp.int32, (768, 768), 1)
    start = row - 20
    own_sums = jnp.where((col >= start) & (col < row), sums, 0.0).astype(BF)
    in_chunk = lax.broadcasted_iota(jnp.int32, (768, 1), 0)
    in_chunk = in_chunk - (in_chunk * 2731 >> 16) * 24
    lane = lax.broadcasted_iota(jnp.int32, (768, 640), 1)
    spread = jnp.where(lane == in_chunk, 1.0, 0.0).astype(BF)
    bias = dot(own_sums, spread)
    out_ref[...] = jnp.where(in_chunk == 20, bias, part).astype(BF)


def home_kernel(got_ref, dst_ref, weight_ref, bias_ref, branch_ref, grad_ref):
    rows = dot(rows_at(dst_ref[...], 1024), got_ref[...], 0, 0).astype(BF)
    att = jnp.concatenate([rows[:128], rows[512:640]], axis=1)
    branch_ref[...] = (dot(att, weight_ref[...]) + bias_ref[...].astype(F32)).astype(BF)
    grad_ref[...] = jnp.concatenate(
        [rows[(t * 4 + g) * 128:(t * 4 + g + 1) * 128] for g in range(1, 4) for t in range(2)], axis=1
    )


def picked_columns():
    col = np.arange(768)
    t, sp, j = col // 384, (col % 384) // 24, col % 24
    return np.where(j < 20, sp * 40 + t * 20 + j, -1).astype(np.int32)[None]


def body(qkv, out_grad, block_image, proj_weight, proj_bias):
    own_sp, own_tp = lax.axis_index("sp"), lax.axis_index("tp")
    dp_count = lax.axis_size("dp")
    images = block_image[0]
    index = jnp.arange(64, dtype=jnp.int32)
    alike = (images[:, None] == images[None, :]) & (index[:, None] != index[None, :])
    twin = jnp.any(alike, axis=1)
    twin_row = jnp.any(alike, axis=0)
    before = index[None, :] < index[:, None]
    rank = jnp.sum((before & (twin_row[None, :] == twin[:, None])).astype(jnp.int32), axis=1)
    twins = jnp.sum(twin.astype(jnp.int32))
    place = jnp.where(twin, rank, twins + rank)
    is_double = (2 * own_sp < twins).astype(jnp.int32)[None]
    four = jnp.arange(4, dtype=jnp.int32)
    two = jnp.arange(2, dtype=jnp.int32)
    dst = (
        ((place >> 1) * 32 + (place & 1) * 2)[None, None, :, None]
        + two[:, None, None, None] * 16
        + four[None, :, None, None] * 4
        + two[None, None, None, :]
    ).reshape(1, 1024)
    qkv_rows = qkv.reshape(128, 1920)
    grad_rows = out_grad.reshape(128, 1280)
    outgoing = call(
        send_kernel, arr((1024, 512), BF), [VM] * 5,
        qkv_rows, grad_rows, proj_weight, dst, jnp.asarray(picked_columns()),
    )
    arrived = lax.all_to_all(
        outgoing.reshape(64, 16, 512), ("sp", "tp"), split_axis=0, concat_axis=0, tiled=True
    ).reshape(1024, 512)
    attended, probs, ordered = call(
        attend_kernel, (arr((256, 320), BF), arr((1024, 256), F32), arr((1024, 512), BF)), [SM, VM],
        is_double, arrived,
    )
    other = lax.ppermute(attended, "tp", [(0, 1), (1, 0)])
    returning = call(back_kernel, arr((1024, 320), BF), [VM] * 3, ordered, probs, attended)
    core = own_tp.astype(jnp.int32)[None]
    part = call(weight_kernel, arr((768, 640), BF), [SM, VM, VM, VM], core, ordered, attended, other)
    shares = lax.all_to_all(part.reshape(32, 24, 640), "sp", split_axis=0, concat_axis=0, tiled=True)
    share = jnp.sum(shares.astype(F32), axis=0).astype(BF)
    spread = jnp.broadcast_to(share[None], (dp_count, 24, 640))
    totals = lax.all_to_all(spread, "dp", split_axis=0, concat_axis=0, tiled=True)
    total = jnp.sum(totals.astype(F32), axis=0) * ((dp_count * 8192) ** -0.5)
    returned = lax.all_to_all(
        returning.reshape(64, 16, 320), ("sp", "tp"), split_axis=0, concat_axis=0, tiled=True
    ).reshape(1024, 320)
    branch, qkv_grad = call(
        home_kernel, (arr((128, 1280), BF), arr((128, 1920), BF)), [VM] * 4,
        returned, dst, proj_weight, proj_bias.reshape(1, 1280),
    )
    return (
        branch.reshape(1, 64, 2, 1280),
        qkv_grad.reshape(1, 64, 2, 1920),
        total[:20].T,
        total[20, :20],
    )


def solution(mesh):
    in_specs = (
        P("dp", None, ("sp", "tp"), None),
        P("dp", None, ("sp", "tp"), None),
        P("dp", None),
        P(),
        P(),
    )
    out_specs = (
        P("dp", None, ("sp", "tp"), None),
        P("dp", None, ("sp", "tp"), None),
        P(None, ("sp", "tp")),
        P(("sp", "tp")),
    )
    return jax.shard_map(body, mesh=mesh, in_specs=in_specs, out_specs=out_specs, check_vma=False)
```

```python
import jax
import jax.numpy as jnp
import numpy as np
from jax import lax
from jax.experimental import pallas as pl
from jax.experimental.pallas import tpu as pltpu
from jax.sharding import PartitionSpec as P

HD = 80
BF = jnp.bfloat16
F32 = jnp.float32
masked_score = -1e30

VM = pl.BlockSpec(memory_space=pltpu.VMEM)
SM = pl.BlockSpec(memory_space=pltpu.SMEM)
PARAMS = pltpu.CompilerParams(vmem_limit_bytes=20 * 1024 * 1024)


def dot(a, b, ca=1, cb=0):
    return lax.dot_general(a, b, (((ca,), (cb,)), ((), ())), preferred_element_type=F32)


def call(kernel, outs, specs, *args):
    return pl.pallas_call(
        kernel,
        out_shape=outs,
        in_specs=specs,
        out_specs=jax.tree.map(lambda _: VM, outs),
        compiler_params=PARAMS,
    )(*args)


def arr(shape, dtype):
    return jax.ShapeDtypeStruct(shape, dtype)


def rows_at(row_of, count):
    n = row_of.shape[1]
    return jnp.where(lax.broadcasted_iota(jnp.int32, (count, n), 0) == row_of, 1.0, 0.0).astype(BF)


def slot_rows(shape, dim):
    i = lax.broadcasted_iota(jnp.int32, shape, dim)
    return ((i >> 2) & 3) * 256 + ((i >> 1) & 1) * 128 + (i >> 4) * 2 + (i & 1)


def placement(image_row):
    row = lax.broadcasted_iota(jnp.int32, (64, 64), 0)
    col = lax.broadcasted_iota(jnp.int32, (64, 64), 1)
    image_rows = jnp.broadcast_to(image_row, (64, 64))
    image_col = jnp.sum(jnp.where(row == col, image_rows, 0), axis=1, keepdims=True)
    alike = jnp.where((image_col == image_rows) & (row != col), 1.0, 0.0)
    twin_col = jnp.sum(alike, axis=1, keepdims=True)
    twin_row = jnp.sum(alike, axis=0, keepdims=True)
    rank = jnp.sum(jnp.where((row < col) & (twin_col == twin_row), 1.0, 0.0), axis=0, keepdims=True)
    twins = jnp.sum(twin_row, axis=1, keepdims=True)
    place = rank + jnp.where(twin_row > 0, 0.0, twins)
    lane = lax.broadcasted_iota(jnp.int32, (64, 1024), 1)
    block = lax.broadcasted_iota(jnp.int32, (64, 1024), 0)
    widen = jnp.where(((lane >> 1) & 63) == block, 1.0, 0.0).astype(BF)
    wide = dot(jnp.broadcast_to(place, (8, 64)).astype(BF), widen).astype(jnp.int32)
    lane = lax.broadcasted_iota(jnp.int32, (8, 1024), 1)
    dst = (wide >> 1) * 32 + ((lane >> 9) & 1) * 16 + ((lane >> 7) & 3) * 4 + (wide & 1) * 2 + (lane & 1)
    return dst, jnp.broadcast_to(twins, (8, 1024)).astype(jnp.int32)


def send_kernel(qkv_ref, grad_ref, weight_ref, image_ref, pick_ref, out_ref, info_ref):
    dst, twins = placement(image_ref[...])
    info_ref[...] = jnp.concatenate([dst, twins], axis=0)
    grad = grad_ref[...]
    delta = dot(grad, weight_ref[...], 1, 1).astype(BF)
    pick = rows_at(pick_ref[...], 640)
    low = dot(grad[:, :640], pick).astype(BF)
    high = dot(grad[:, 640:], pick).astype(BF)
    blocks = []
    for t in range(2):
        picked = jnp.concatenate([low[:, t * 384:(t + 1) * 384], high[:, t * 384:(t + 1) * 384]], axis=1)
        for g in range(4):
            if g < 3:
                at = g * 640 + t * 320
                kind = qkv_ref[:, at:at + 320]
            else:
                kind = delta[:, t * 320:(t + 1) * 320]
            blocks.append(jnp.concatenate([kind, picked[:, g * 192:(g + 1) * 192]], axis=1))
    stack = jnp.concatenate(blocks, axis=0)
    out_ref[...] = dot(rows_at(dst[:1], 1024), stack).astype(BF)


def head_masks(rows):
    lane = lax.broadcasted_iota(jnp.int32, (rows, 320), 1)
    return [(lane >= h * HD) & (lane < (h + 1) * HD) for h in range(4)]


def by_head(x, masks):
    zero = jnp.zeros_like(x)
    return jnp.concatenate([jnp.where(m, x, zero) for m in masks], axis=0)


def own_head(x, masks):
    total = jnp.zeros((256, 320), F32)
    for h, m in enumerate(masks):
        total = jnp.where(m, x[h * 256:(h + 1) * 256], total)
    return total


def attend_kernel(own_ref, info_ref, got_ref, att_ref, probs_ref, sorted_ref):
    sel = rows_at(slot_rows((1, 1024), 1), 1024)
    rows = dot(sel, got_ref[...]).astype(BF)
    sorted_ref[...] = rows
    query, key, value = rows[:256, :320], rows[256:512, :320], rows[512:768, :320]
    masks = head_masks(256)
    scores = dot(by_head(query, masks), key, 1, 1) * (HD ** -0.5)
    row = lax.broadcasted_iota(jnp.int32, (1024, 256), 0)
    col = lax.broadcasted_iota(jnp.int32, (1024, 256), 1)
    twins = info_ref[8:9, :256]
    apart = (((row ^ col) >> 7) & 1) > jnp.where(2 * own_ref[0] < twins, 1, 0)
    scores = jnp.where(apart, masked_score, scores)
    exp_scores = jnp.exp(scores - jnp.max(scores, axis=-1, keepdims=True))
    probs = exp_scores / jnp.sum(exp_scores, axis=-1, keepdims=True)
    probs_ref[...] = probs
    att_ref[...] = own_head(dot(probs.astype(BF), value), masks).astype(BF)


def back_kernel(sorted_ref, probs_ref, att_ref, out_ref):
    rows = sorted_ref[...]
    query, key = rows[:256, :320], rows[256:512, :320]
    value, delta = rows[512:768, :320], rows[768:, :320]
    masks = head_masks(256)
    query_heads, delta_heads = by_head(query, masks), by_head(delta, masks)
    probs = probs_ref[...]
    prob_grad = dot(delta_heads, value, 1, 1)
    centre = jnp.sum(probs * prob_grad, axis=-1, keepdims=True)
    score_grad = (probs * (prob_grad - centre) * (HD ** -0.5)).astype(BF)
    query_grad = own_head(dot(score_grad, key), masks).astype(BF)
    key_grad = dot(score_grad, query_heads, 0, 0).astype(BF)
    value_grad = dot(probs.astype(BF), delta_heads, 0, 0).astype(BF)
    stack = jnp.concatenate([att_ref[...], query_grad, key_grad, value_grad], axis=0)
    lane = lax.broadcasted_iota(jnp.int32, (1024, 1024), 1)
    back = jnp.where(lane == slot_rows((1024, 1), 0), 1.0, 0.0).astype(BF)
    out_ref[...] = dot(back, stack).astype(BF)


def weight_kernel(core_ref, sorted_ref, own_ref, other_ref, out_ref):
    rows = sorted_ref[...]
    grad = jnp.concatenate([rows[g * 256:(g + 1) * 256, 320:] for g in range(4)], axis=1)
    first = core_ref[0] == 0
    own, other = own_ref[...], other_ref[...]
    att = jnp.concatenate([jnp.where(first, own, other), jnp.where(first, other, own)], axis=1)
    part = dot(grad, att, 0, 0)
    sums = dot(jnp.ones((8, 256), BF), grad)[:1]
    row = lax.broadcasted_iota(jnp.int32, (768, 768), 0)
    col = lax.broadcasted_iota(jnp.int32, (768, 768), 1)
    start = row - 20
    own_sums = jnp.where((col >= start) & (col < row), sums, 0.0).astype(BF)
    in_chunk = lax.broadcasted_iota(jnp.int32, (768, 1), 0)
    in_chunk = in_chunk - (in_chunk * 2731 >> 16) * 24
    lane = lax.broadcasted_iota(jnp.int32, (768, 640), 1)
    spread = jnp.where(lane == in_chunk, 1.0, 0.0).astype(BF)
    bias = dot(own_sums, spread)
    out_ref[...] = jnp.where(in_chunk == 20, bias, part).astype(BF)


def home_kernel(got_ref, info_ref, weight_ref, bias_ref, branch_ref, grad_ref):
    rows = dot(rows_at(info_ref[:1, :], 1024), got_ref[...], 0, 0).astype(BF)
    att = jnp.concatenate([rows[:128], rows[512:640]], axis=1)
    branch_ref[...] = (dot(att, weight_ref[...]) + bias_ref[...].astype(F32)).astype(BF)
    grad_ref[...] = jnp.concatenate(
        [rows[(t * 4 + g) * 128:(t * 4 + g + 1) * 128] for g in range(1, 4) for t in range(2)], axis=1
    )


def picked_columns():
    col = np.arange(768)
    t, sp, j = col // 384, (col % 384) // 24, col % 24
    return np.where(j < 20, sp * 40 + t * 20 + j, -1).astype(np.int32)[None]


def body(qkv, out_grad, block_image, proj_weight, proj_bias):
    own_sp, own_tp = lax.axis_index("sp"), lax.axis_index("tp")
    dp_count = lax.axis_size("dp")
    qkv_rows = qkv.reshape(128, 1920)
    grad_rows = out_grad.reshape(128, 1280)
    outgoing, info = call(
        send_kernel, (arr((1024, 512), BF), arr((16, 1024), jnp.int32)), [VM] * 5,
        qkv_rows, grad_rows, proj_weight, block_image, jnp.asarray(picked_columns()),
    )
    arrived = lax.all_to_all(
        outgoing.reshape(64, 16, 512), ("sp", "tp"), split_axis=0, concat_axis=0, tiled=True
    ).reshape(1024, 512)
    attended, probs, ordered = call(
        attend_kernel, (arr((256, 320), BF), arr((1024, 256), F32), arr((1024, 512), BF)), [SM, VM, VM],
        own_sp.astype(jnp.int32)[None], info, arrived,
    )
    other = lax.ppermute(attended, "tp", [(0, 1), (1, 0)])
    returning = call(back_kernel, arr((1024, 320), BF), [VM] * 3, ordered, probs, attended)
    core = own_tp.astype(jnp.int32)[None]
    part = call(weight_kernel, arr((768, 640), BF), [SM, VM, VM, VM], core, ordered, attended, other)
    shares = lax.all_to_all(part.reshape(32, 24, 640), "sp", split_axis=0, concat_axis=0, tiled=True)
    share = jnp.sum(shares.astype(F32), axis=0).astype(BF)
    totals = lax.all_gather(share, "dp")
    total = jnp.sum(totals.astype(F32), axis=0) * ((dp_count * 8192) ** -0.5)
    returned = lax.all_to_all(
        returning.reshape(64, 16, 320), ("sp", "tp"), split_axis=0, concat_axis=0, tiled=True
    ).reshape(1024, 320)
    branch, qkv_grad = call(
        home_kernel, (arr((128, 1280), BF), arr((128, 1920), BF)), [VM] * 4,
        returned, info, proj_weight, proj_bias.reshape(1, 1280),
    )
    return (
        branch.reshape(1, 64, 2, 1280),
        qkv_grad.reshape(1, 64, 2, 1920),
        total[:20].T,
        total[20, :20],
    )


def solution(mesh):
    in_specs = (
        P("dp", None, ("sp", "tp"), None),
        P("dp", None, ("sp", "tp"), None),
        P("dp", None),
        P(),
        P(),
    )
    out_specs = (
        P("dp", None, ("sp", "tp"), None),
        P("dp", None, ("sp", "tp"), None),
        P(None, ("sp", "tp")),
        P(("sp", "tp")),
    )
    return jax.shard_map(body, mesh=mesh, in_specs=in_specs, out_specs=out_specs, check_vma=False)
```

```python
import functools

import jax
import jax.numpy as jnp
import numpy as np
from jax import lax
from jax.experimental import pallas as pl
from jax.experimental.pallas import tpu as pltpu
from jax.sharding import PartitionSpec as P

HD = 80
BF = jnp.bfloat16
F32 = jnp.float32
masked_score = -1e30

VM = pl.BlockSpec(memory_space=pltpu.VMEM)
SM = pl.BlockSpec(memory_space=pltpu.SMEM)
PARAMS = pltpu.CompilerParams(vmem_limit_bytes=20 * 1024 * 1024)


def dot(a, b, ca=1, cb=0):
    return lax.dot_general(a, b, (((ca,), (cb,)), ((), ())), preferred_element_type=F32)


def call(kernel, outs, specs, *args):
    return pl.pallas_call(
        kernel,
        out_shape=outs,
        in_specs=specs,
        out_specs=jax.tree.map(lambda _: VM, outs),
        compiler_params=PARAMS,
    )(*args)


def arr(shape, dtype):
    return jax.ShapeDtypeStruct(shape, dtype)


def rows_at(row_of, count):
    n = row_of.shape[1]
    return jnp.where(lax.broadcasted_iota(jnp.int32, (count, n), 0) == row_of, 1.0, 0.0).astype(BF)


def slot_rows(shape, dim, bits):
    i = lax.broadcasted_iota(jnp.int32, shape, dim)
    kind = (i >> 2) & ((1 << bits) - 1)
    return kind * 256 + ((i >> 1) & 1) * 128 + (i >> (2 + bits)) * 2 + (i & 1)


def placement(image_row):
    row = lax.broadcasted_iota(jnp.int32, (64, 64), 0)
    col = lax.broadcasted_iota(jnp.int32, (64, 64), 1)
    image_rows = jnp.broadcast_to(image_row, (64, 64))
    image_col = jnp.sum(jnp.where(row == col, image_rows, 0), axis=1, keepdims=True)
    alike = jnp.where((image_col == image_rows) & (row != col), 1.0, 0.0)
    twin_col = jnp.sum(alike, axis=1, keepdims=True)
    twin_row = jnp.sum(alike, axis=0, keepdims=True)
    rank = jnp.sum(jnp.where((row < col) & (twin_col == twin_row), 1.0, 0.0), axis=0, keepdims=True)
    twins = jnp.sum(twin_row, axis=1, keepdims=True)
    place = rank + jnp.where(twin_row > 0, 0.0, twins)
    lane = lax.broadcasted_iota(jnp.int32, (64, 1024), 1)
    block = lax.broadcasted_iota(jnp.int32, (64, 1024), 0)
    widen = jnp.where(((lane >> 1) & 63) == block, 1.0, 0.0).astype(BF)
    wide = dot(jnp.broadcast_to(place, (8, 64)).astype(BF), widen).astype(jnp.int32)
    lane = lax.broadcasted_iota(jnp.int32, (8, 1024), 1)
    dst = (wide >> 1) * 32 + ((lane >> 9) & 1) * 16 + ((lane >> 7) & 3) * 4 + (wide & 1) * 2 + (lane & 1)
    back = (wide >> 1) * 16 + ((lane >> 8) & 1) * 8 + ((lane >> 7) & 1) * 4 + (wide & 1) * 2 + (lane & 1)
    return dst, jnp.broadcast_to(twins, (8, 1024)).astype(jnp.int32), back


def send_kernel(qkv_ref, grad_ref, weight_ref, image_ref, pick_ref, out_ref, info_ref):
    dst, twins, back = placement(image_ref[...])
    info_ref[...] = jnp.concatenate([dst, twins, back], axis=0)
    grad = grad_ref[...]
    delta = dot(grad, weight_ref[...], 1, 1).astype(BF)
    pick = rows_at(pick_ref[...], 640)
    low = dot(grad[:, :640], pick).astype(BF)
    high = dot(grad[:, 640:], pick).astype(BF)
    blocks = []
    for t in range(2):
        parts = [half[:, t * 384 + n * 128:t * 384 + (n + 1) * 128] for n in range(3) for half in (low, high)]
        picked = jnp.concatenate(parts, axis=1)
        for g in range(4):
            if g < 3:
                at = g * 640 + t * 320
                kind = qkv_ref[:, at:at + 320]
            else:
                kind = delta[:, t * 320:(t + 1) * 320]
            blocks.append(jnp.concatenate([kind, picked[:, g * 192:(g + 1) * 192]], axis=1))
    stack = jnp.concatenate(blocks, axis=0)
    out_ref[...] = dot(rows_at(dst[:1], 1024), stack).astype(BF)


def head_masks(rows):
    lane = lax.broadcasted_iota(jnp.int32, (rows, 320), 1)
    return [(lane >= h * HD) & (lane < (h + 1) * HD) for h in range(4)]


def by_head(x, masks):
    zero = jnp.zeros_like(x)
    return jnp.concatenate([jnp.where(m, x, zero) for m in masks], axis=0)


def own_head(x, masks):
    total = jnp.zeros((256, 320), F32)
    for h, m in enumerate(masks):
        total = jnp.where(m, x[h * 256:(h + 1) * 256], total)
    return total


def attend_kernel(own_ref, info_ref, got_ref, att_ref, probs_ref, sorted_ref):
    sel = rows_at(slot_rows((1, 1024), 1, 2), 1024)
    rows = dot(sel, got_ref[...]).astype(BF)
    sorted_ref[...] = rows
    query, key, value = rows[:256, :320], rows[256:512, :320], rows[512:768, :320]
    masks = head_masks(256)
    scores = dot(by_head(query, masks), key, 1, 1) * (HD ** -0.5)
    row = lax.broadcasted_iota(jnp.int32, (1024, 256), 0)
    col = lax.broadcasted_iota(jnp.int32, (1024, 256), 1)
    twins = info_ref[8:9, :256]
    apart = (((row ^ col) >> 7) & 1) > jnp.where(2 * own_ref[0] < twins, 1, 0)
    scores = jnp.where(apart, masked_score, scores)
    exp_scores = jnp.exp(scores - jnp.max(scores, axis=-1, keepdims=True))
    probs = exp_scores / jnp.sum(exp_scores, axis=-1, keepdims=True)
    probs_ref[...] = probs
    att_ref[...] = own_head(dot(probs.astype(BF), value), masks).astype(BF)


def back_kernel(sorted_ref, probs_ref, att_ref, out_ref):
    rows = sorted_ref[...]
    query, key = rows[:256, :320], rows[256:512, :320]
    value, delta = rows[512:768, :320], rows[768:, :320]
    masks = head_masks(256)
    query_heads, delta_heads = by_head(query, masks), by_head(delta, masks)
    probs = probs_ref[...]
    prob_grad = dot(delta_heads, value, 1, 1)
    centre = jnp.sum(probs * prob_grad, axis=-1, keepdims=True)
    score_grad = (probs * (prob_grad - centre) * (HD ** -0.5)).astype(BF)
    query_grad = own_head(dot(score_grad, key), masks).astype(BF)
    key_grad = dot(score_grad, query_heads, 0, 0).astype(BF)
    value_grad = dot(probs.astype(BF), delta_heads, 0, 0).astype(BF)
    stack = jnp.concatenate(
        [
            jnp.concatenate([att_ref[...], query_grad], axis=1),
            jnp.concatenate([key_grad, value_grad], axis=1),
        ],
        axis=0,
    )
    lane = lax.broadcasted_iota(jnp.int32, (512, 512), 1)
    back = jnp.where(lane == slot_rows((512, 1), 0, 1), 1.0, 0.0).astype(BF)
    out_ref[...] = dot(back, stack).astype(BF)


def weight_kernel(core_ref, sorted_ref, own_ref, other_ref, out_ref):
    rows = sorted_ref[...]
    grad = jnp.concatenate([rows[g * 256:(g + 1) * 256, 320:] for g in range(4)], axis=1)
    first = core_ref[0] == 0
    own, other = own_ref[...], other_ref[...]
    att = jnp.concatenate([jnp.where(first, own, other), jnp.where(first, other, own)], axis=1)
    part = dot(grad, att, 0, 0)
    odd = (lax.broadcasted_iota(jnp.int32, (256, 320), 0) & 1) == 1
    rest = jnp.where(odd, part[512:, 320:], part[512:, :320])
    sums = dot(jnp.ones((8, 256), BF), grad)[:1]
    row = lax.broadcasted_iota(jnp.int32, (256, 768), 0)
    col = lax.broadcasted_iota(jnp.int32, (256, 768), 1)
    own_sums = jnp.where(((col >> 3) & 31) == (row >> 3), sums, 0.0).astype(BF)
    k = lax.broadcasted_iota(jnp.int32, (768, 64), 0)
    lane = lax.broadcasted_iota(jnp.int32, (768, 64), 1)
    at = jnp.where(k < 512, (k >> 8) * 8 + (k & 7), 16 + ((k & 7) >> 1))
    spread = jnp.where((lane == at) & ((k < 512) | ((k & 1) == 0)), 1.0, 0.0).astype(BF)
    bias = dot(own_sums, spread)
    out_ref[...] = jnp.concatenate([part[:256], part[256:512], rest, bias], axis=1).astype(BF)


def total_kernel(scale, got_ref, weight_ref, bias_ref):
    total = got_ref[0].astype(F32)
    for n in range(1, got_ref.shape[0]):
        total = total + got_ref[n].astype(F32)
    total = total * scale
    weight_ref[0:8, :] = total[:, :640]
    weight_ref[8:16, :] = total[:, 640:1280]
    for n in range(4):
        weight_ref[16 + n:17 + n, 0:320] = total[2 * n:2 * n + 1, 1280:1600]
        weight_ref[16 + n:17 + n, 320:640] = total[2 * n + 1:2 * n + 2, 1280:1600]
    bias_ref[...] = total[:1, 1600:]


def home_kernel(got_ref, info_ref, weight_ref, bias_ref, branch_ref, grad_ref):
    rows = dot(rows_at(info_ref[16:17, :512], 512), got_ref[...], 0, 0).astype(BF)
    att = jnp.concatenate([rows[:128, :320], rows[256:384, :320]], axis=1)
    branch_ref[...] = (dot(att, weight_ref[...]) + bias_ref[...].astype(F32)).astype(BF)
    grad_ref[...] = jnp.concatenate(
        [
            rows[(t * 2 + p) * 128:(t * 2 + p + 1) * 128, n * 320:(n + 1) * 320]
            for p, n in ((0, 1), (1, 0), (1, 1))
            for t in range(2)
        ],
        axis=1,
    )


def picked_columns():
    col = np.arange(768)
    t, group, sp, r = col // 384, (col // 128) % 3, (col // 8) % 16, col % 8
    return (sp * 40 + t * 20 + np.where(group < 2, group * 8 + r, 16 + r // 2)).astype(np.int32)[None]


def body(qkv, out_grad, block_image, proj_weight, proj_bias):
    own_sp, own_tp = lax.axis_index("sp"), lax.axis_index("tp")
    dp_count = lax.axis_size("dp")
    qkv_rows = qkv.reshape(128, 1920)
    grad_rows = out_grad.reshape(128, 1280)
    outgoing, info = call(
        send_kernel, (arr((1024, 512), BF), arr((24, 1024), jnp.int32)), [VM] * 5,
        qkv_rows, grad_rows, proj_weight, block_image, jnp.asarray(picked_columns()),
    )
    arrived = lax.all_to_all(
        outgoing.reshape(64, 16, 512), ("sp", "tp"), split_axis=0, concat_axis=0, tiled=True
    ).reshape(1024, 512)
    attended, probs, ordered = call(
        attend_kernel, (arr((256, 320), BF), arr((1024, 256), F32), arr((1024, 512), BF)), [SM, VM, VM],
        own_sp.astype(jnp.int32)[None], info, arrived,
    )
    other = lax.ppermute(attended, "tp", [(0, 1), (1, 0)])
    returning = call(back_kernel, arr((512, 640), BF), [VM] * 3, ordered, probs, attended)
    core = own_tp.astype(jnp.int32)[None]
    part = call(weight_kernel, arr((256, 1664), BF), [SM, VM, VM, VM], core, ordered, attended, other)
    shares = lax.all_to_all(part.reshape(32, 8, 1664), "sp", split_axis=0, concat_axis=0, tiled=True)
    share = jnp.sum(shares.astype(F32), axis=0).astype(BF)
    share, returning = lax.optimization_barrier((share, returning))
    totals = lax.all_gather(share, "dp")
    total, sums = call(
        functools.partial(total_kernel, (dp_count * 8192) ** -0.5),
        (arr((20, 640), F32), arr((1, 64), F32)), [VM], totals,
    )
    returned = lax.all_to_all(
        returning.reshape(64, 8, 640), ("sp", "tp"), split_axis=0, concat_axis=0, tiled=True
    ).reshape(512, 640)
    branch, qkv_grad = call(
        home_kernel, (arr((128, 1280), BF), arr((128, 1920), BF)), [VM] * 4,
        returned, info, proj_weight, proj_bias.reshape(1, 1280),
    )
    return (
        branch.reshape(1, 64, 2, 1280),
        qkv_grad.reshape(1, 64, 2, 1920),
        total.T,
        sums[0, :20],
    )


def solution(mesh):
    in_specs = (
        P("dp", None, ("sp", "tp"), None),
        P("dp", None, ("sp", "tp"), None),
        P("dp", None),
        P(),
        P(),
    )
    out_specs = (
        P("dp", None, ("sp", "tp"), None),
        P("dp", None, ("sp", "tp"), None),
        P(None, ("sp", "tp")),
        P(("sp", "tp")),
    )
    return jax.shard_map(body, mesh=mesh, in_specs=in_specs, out_specs=out_specs, check_vma=False)
```

```python
import functools

import jax
import jax.numpy as jnp
from jax import lax
from jax.experimental import pallas as pl
from jax.experimental.pallas import tpu as pltpu
from jax.sharding import PartitionSpec as P

HD = 80
BF = jnp.bfloat16
F32 = jnp.float32
masked_score = -1e30

VM = pl.BlockSpec(memory_space=pltpu.VMEM)
SM = pl.BlockSpec(memory_space=pltpu.SMEM)
HBM = pl.BlockSpec(memory_space=pltpu.HBM)
PARAMS = pltpu.CompilerParams(vmem_limit_bytes=20 * 1024 * 1024)
WHOLE = pltpu.CompilerParams(vmem_limit_bytes=60 * 1024 * 1024)


def dot(a, b, ca=1, cb=0):
    return lax.dot_general(a, b, (((ca,), (cb,)), ((), ())), preferred_element_type=F32)


def call(kernel, outs, specs, *args):
    return pl.pallas_call(
        kernel,
        out_shape=outs,
        in_specs=specs,
        out_specs=jax.tree.map(lambda _: VM, outs),
        compiler_params=PARAMS,
    )(*args)


def arr(shape, dtype):
    return jax.ShapeDtypeStruct(shape, dtype)


def rows_at(row_of, count):
    n = row_of.shape[1]
    return jnp.where(lax.broadcasted_iota(jnp.int32, (count, n), 0) == row_of, 1.0, 0.0).astype(BF)


def slot_rows(shape, dim, bits):
    i = lax.broadcasted_iota(jnp.int32, shape, dim)
    kind = (i >> 2) & ((1 << bits) - 1)
    return kind * 64 + ((i >> 1) & 1) * 32 + (i >> (2 + bits)) * 2 + (i & 1)


def placement(image_row):
    row = lax.broadcasted_iota(jnp.int32, (64, 64), 0)
    col = lax.broadcasted_iota(jnp.int32, (64, 64), 1)
    image_rows = jnp.broadcast_to(image_row, (64, 64))
    image_col = jnp.sum(jnp.where(row == col, image_rows, 0), axis=1, keepdims=True)
    alike = jnp.where((image_col == image_rows) & (row != col), 1.0, 0.0)
    twin_col = jnp.sum(alike, axis=1, keepdims=True)
    twin_row = jnp.sum(alike, axis=0, keepdims=True)
    rank = jnp.sum(jnp.where((row < col) & (twin_col == twin_row), 1.0, 0.0), axis=0, keepdims=True)
    twins = jnp.sum(twin_row, axis=1, keepdims=True)
    place = rank + jnp.where(twin_row > 0, 0.0, twins)
    lane = lax.broadcasted_iota(jnp.int32, (64, 512), 1)
    block = lax.broadcasted_iota(jnp.int32, (64, 512), 0)
    widen = jnp.where(((lane >> 1) & 63) == block, 1.0, 0.0).astype(BF)
    wide = dot(jnp.broadcast_to(place, (8, 64)).astype(BF), widen).astype(jnp.int32)
    lane = lax.broadcasted_iota(jnp.int32, (8, 512), 1)
    base = (wide >> 1) * 16 + (wide & 1) * 2 + (lane & 1)
    dst = base + ((lane >> 7) & 3) * 4
    back = base + ((lane >> 8) & 1) * 8 + ((lane >> 7) & 1) * 4
    return dst, jnp.broadcast_to(twins, (8, 512)).astype(jnp.int32), back


def picked_columns():
    k = lax.broadcasted_iota(jnp.int32, (1, 768), 1)
    t = jnp.where(k >= 384, 1, 0)
    k = k - 384 * t
    return ((k >> 3) & 15) * 40 + t * 20 + jnp.where(k < 256, (k >> 7) * 8 + (k & 7), 16 + ((k & 7) >> 1))


def send_kernel(
    qkv_hbm, grad_hbm, weight_hbm, image_hbm, out_ref, info_ref, qkv_ref, grad_ref, weight_ref, image_ref, sems
):
    pairs = ((image_hbm, image_ref), (grad_hbm, grad_ref), (qkv_hbm, qkv_ref), (weight_hbm, weight_ref))
    copies = [pltpu.make_async_copy(a, b, sems.at[n]) for n, (a, b) in enumerate(pairs)]
    for copy in copies:
        copy.start()
    pick = rows_at(picked_columns(), 640)
    copies[0].wait()
    dst, twins, back = placement(image_ref[...])
    info_ref[...] = jnp.concatenate([dst, twins, back], axis=0)
    move = rows_at(dst[:1], 512)
    copies[1].wait()
    grad = grad_ref[...].reshape(128, 1280)
    low = dot(grad[:, :640], pick).astype(BF)
    high = dot(grad[:, 640:], pick).astype(BF)
    copies[2].wait()
    qkv = qkv_ref[...].reshape(128, 1920)
    copies[3].wait()
    delta = dot(grad, weight_ref[...], 1, 1).astype(BF)
    for t in range(2):
        parts = [half[:, t * 384 + n * 128:t * 384 + (n + 1) * 128] for n in range(3) for half in (low, high)]
        picked = jnp.concatenate(parts, axis=1)
        blocks = []
        for g in range(4):
            if g < 3:
                kind = qkv[:, g * 640 + t * 320:g * 640 + (t + 1) * 320]
            else:
                kind = delta[:, t * 320:(t + 1) * 320]
            blocks.append(jnp.concatenate([kind, picked[:, g * 192:(g + 1) * 192]], axis=1))
        stack = jnp.concatenate(blocks, axis=0)
        out_ref[:, t] = dot(move, stack).astype(BF).reshape(32, 16, 512)


def head_masks(rows):
    lane = lax.broadcasted_iota(jnp.int32, (rows, 320), 1)
    return [(lane >= h * HD) & (lane < (h + 1) * HD) for h in range(4)]


def by_head(x, masks):
    zero = jnp.zeros_like(x)
    return jnp.concatenate([jnp.where(m, x, zero) for m in masks], axis=0)


def own_head(x, masks):
    total = jnp.zeros((256, 320), F32)
    for h, m in enumerate(masks):
        total = jnp.where(m, x[h * 256:(h + 1) * 256], total)
    return total


def attend_kernel(own_ref, info_ref, got_ref, att_ref, probs_ref, sorted_ref):
    sel = rows_at(slot_rows((1, 256), 1, 2), 256)
    quarters = [dot(sel, got_ref[n * 256:(n + 1) * 256, :]).astype(BF) for n in range(4)]
    kinds = [jnp.concatenate([x[g * 64:(g + 1) * 64] for x in quarters], axis=0) for g in range(4)]
    for g in range(4):
        sorted_ref[g * 256:(g + 1) * 256, :] = kinds[g]
    query, key, value = kinds[0][:, :320], kinds[1][:, :320], kinds[2][:, :320]
    masks = head_masks(256)
    scores = dot(by_head(query, masks), key, 1, 1) * (HD ** -0.5)
    row = lax.broadcasted_iota(jnp.int32, (256, 256), 0)
    col = lax.broadcasted_iota(jnp.int32, (256, 256), 1)
    twins = info_ref[8:9, :256]
    apart = (((row ^ col) >> 5) & 1) > jnp.where(2 * own_ref[0] < twins, 1, 0)
    probs_bf = []
    for h in range(4):
        own = jnp.where(apart, masked_score, scores[h * 256:(h + 1) * 256])
        exp_scores = jnp.exp(own - jnp.max(own, axis=-1, keepdims=True))
        probs = exp_scores / jnp.sum(exp_scores, axis=-1, keepdims=True)
        probs_ref[h * 256:(h + 1) * 256, :] = probs
        probs_bf.append(probs.astype(BF))
    att_ref[...] = own_head(dot(jnp.concatenate(probs_bf, axis=0), value), masks).astype(BF)


def back_kernel(sorted_ref, probs_ref, att_ref, out_ref):
    rows = sorted_ref[...]
    query, key = rows[:256, :320], rows[256:512, :320]
    value, delta = rows[512:768, :320], rows[768:, :320]
    masks = head_masks(256)
    query_heads, delta_heads = by_head(query, masks), by_head(delta, masks)
    probs = probs_ref[...]
    prob_grad = dot(delta_heads, value, 1, 1)
    centre = jnp.sum(probs * prob_grad, axis=-1, keepdims=True)
    score_grad = (probs * (prob_grad - centre) * (HD ** -0.5)).astype(BF)
    query_grad = own_head(dot(score_grad, key), masks).astype(BF)
    key_grad = dot(score_grad, query_heads, 0, 0).astype(BF)
    value_grad = dot(probs.astype(BF), delta_heads, 0, 0).astype(BF)
    first = jnp.concatenate([att_ref[...], query_grad], axis=1)
    second = jnp.concatenate([key_grad, value_grad], axis=1)
    lane = lax.broadcasted_iota(jnp.int32, (128, 128), 1)
    back = jnp.where(lane == slot_rows((128, 1), 0, 1), 1.0, 0.0).astype(BF)
    for n in range(4):
        stack = jnp.concatenate([first[n * 64:(n + 1) * 64], second[n * 64:(n + 1) * 64]], axis=0)
        out_ref[n * 128:(n + 1) * 128, :] = dot(back, stack).astype(BF)


def weight_kernel(core_ref, sorted_ref, own_ref, other_ref, out_ref):
    rows = sorted_ref[...]
    grad = jnp.concatenate([rows[g * 256:(g + 1) * 256, 320:] for g in range(4)], axis=1)
    first = core_ref[0] == 0
    own, other = own_ref[...], other_ref[...]
    att = jnp.concatenate([jnp.where(first, own, other), jnp.where(first, other, own)], axis=1)
    part = dot(grad, att, 0, 0)
    odd = (lax.broadcasted_iota(jnp.int32, (256, 320), 0) & 1) == 1
    rest = jnp.where(odd, part[512:, 320:], part[512:, :320])
    sums = dot(jnp.ones((8, 256), BF), grad)[:1]
    row = lax.broadcasted_iota(jnp.int32, (256, 768), 0)
    col = lax.broadcasted_iota(jnp.int32, (256, 768), 1)
    own_sums = jnp.where(((col >> 3) & 31) == (row >> 3), sums, 0.0).astype(BF)
    k = lax.broadcasted_iota(jnp.int32, (768, 64), 0)
    lane = lax.broadcasted_iota(jnp.int32, (768, 64), 1)
    at = jnp.where(k < 512, (k >> 8) * 8 + (k & 7), 16 + ((k & 7) >> 1))
    spread = jnp.where((lane == at) & ((k < 512) | ((k & 1) == 0)), 1.0, 0.0).astype(BF)
    bias = dot(own_sums, spread)
    out_ref[...] = jnp.concatenate([part[:256], part[256:512], rest, bias], axis=1).astype(BF)


def total_kernel(scale, got_ref, weight_ref, bias_ref):
    total = got_ref[0].astype(F32)
    for n in range(1, got_ref.shape[0]):
        total = total + got_ref[n].astype(F32)
    total = total * scale
    weight_ref[0:8, :] = total[:, :640]
    weight_ref[8:16, :] = total[:, 640:1280]
    for n in range(4):
        weight_ref[16 + n:17 + n, 0:320] = total[2 * n:2 * n + 1, 1280:1600]
        weight_ref[16 + n:17 + n, 320:640] = total[2 * n + 1:2 * n + 2, 1280:1600]
    bias_ref[...] = total[:1, 1600:]


def home_kernel(got_ref, info_ref, weight_ref, bias_ref, branch_ref, grad_ref):
    rows = dot(rows_at(info_ref[16:17, :], 512), got_ref[...], 0, 0).astype(BF)
    att = jnp.concatenate([rows[:128, :320], rows[256:384, :320]], axis=1)
    branch = dot(att, weight_ref[...]) + bias_ref[...].astype(F32)
    branch_ref[...] = branch.astype(BF).reshape(64, 2, 1280)
    for n, (p, m) in enumerate(((0, 1), (1, 0), (1, 1))):
        both = [rows[(t * 2 + p) * 128:(t * 2 + p + 1) * 128, m * 320:(m + 1) * 320] for t in range(2)]
        grad_ref[:, :, n * 640:(n + 1) * 640] = jnp.concatenate(both, axis=1).reshape(64, 2, 640)


def body(qkv, out_grad, block_image, proj_weight, proj_bias):
    own_sp, own_tp = lax.axis_index("sp"), lax.axis_index("tp")
    dp_count = lax.axis_size("dp")
    outgoing, info = pl.pallas_call(
        send_kernel,
        out_shape=(arr((32, 2, 16, 512), BF), arr((24, 512), jnp.int32)),
        in_specs=[HBM] * 4,
        out_specs=(VM, VM),
        scratch_shapes=[
            pltpu.VMEM((64, 2, 1920), BF),
            pltpu.VMEM((64, 2, 1280), BF),
            pltpu.VMEM((640, 1280), BF),
            pltpu.VMEM((1, 64), jnp.int32),
            pltpu.SemaphoreType.DMA((4,)),
        ],
        compiler_params=WHOLE,
    )(qkv[0], out_grad[0], proj_weight, block_image)
    arrived = lax.all_to_all(
        outgoing.reshape(64, 16, 512), ("sp", "tp"), split_axis=0, concat_axis=0, tiled=True
    ).reshape(1024, 512)
    attended, probs, ordered = call(
        attend_kernel, (arr((256, 320), BF), arr((1024, 256), F32), arr((1024, 512), BF)), [SM, VM, VM],
        own_sp.astype(jnp.int32)[None], info, arrived,
    )
    other = lax.ppermute(attended, "tp", [(0, 1), (1, 0)])
    returning = call(back_kernel, arr((512, 640), BF), [VM] * 3, ordered, probs, attended)
    core = own_tp.astype(jnp.int32)[None]
    part = call(weight_kernel, arr((256, 1664), BF), [SM, VM, VM, VM], core, ordered, attended, other)
    shares = lax.all_to_all(part.reshape(32, 8, 1664), "sp", split_axis=0, concat_axis=0, tiled=True)
    share = jnp.sum(shares.astype(F32), axis=0).astype(BF)
    share, returning = lax.optimization_barrier((share, returning))
    count = dp_count // 4
    near = [[4 * n + m for m in range(4)] for n in range(count)]
    far = [[4 * n + m for n in range(count)] for m in range(4)]
    fours = lax.all_gather(share, "dp", axis_index_groups=near)
    fours = jnp.sum(fours.astype(F32), axis=0).astype(BF)
    totals = lax.all_gather(fours, "dp", axis_index_groups=far)
    total, sums = call(
        functools.partial(total_kernel, (dp_count * 8192) ** -0.5),
        (arr((20, 640), F32), arr((1, 64), F32)), [VM], totals,
    )
    returned = lax.all_to_all(
        returning.reshape(64, 8, 640), ("sp", "tp"), split_axis=0, concat_axis=0, tiled=True
    ).reshape(512, 640)
    branch, qkv_grad = call(
        home_kernel, (arr((64, 2, 1280), BF), arr((64, 2, 1920), BF)), [VM] * 4,
        returned, info, proj_weight, proj_bias.reshape(1, 1280),
    )
    return (
        branch[None],
        qkv_grad[None],
        total.T,
        sums[0, :20],
    )


def solution(mesh):
    in_specs = (
        P("dp", None, ("sp", "tp"), None),
        P("dp", None, ("sp", "tp"), None),
        P("dp", None),
        P(),
        P(),
    )
    out_specs = (
        P("dp", None, ("sp", "tp"), None),
        P("dp", None, ("sp", "tp"), None),
        P(None, ("sp", "tp")),
        P(("sp", "tp")),
    )
    return jax.shard_map(body, mesh=mesh, in_specs=in_specs, out_specs=out_specs, check_vma=False)
```

```python
import functools

import jax
import jax.numpy as jnp
from jax import lax
from jax.experimental import pallas as pl
from jax.experimental.pallas import tpu as pltpu
from jax.sharding import PartitionSpec as P

HD = 80
BF = jnp.bfloat16
F32 = jnp.float32
masked_score = -1e30

VM = pl.BlockSpec(memory_space=pltpu.VMEM)
SM = pl.BlockSpec(memory_space=pltpu.SMEM)
HBM = pl.BlockSpec(memory_space=pltpu.HBM)
PARAMS = pltpu.CompilerParams(vmem_limit_bytes=20 * 1024 * 1024)
WHOLE = pltpu.CompilerParams(vmem_limit_bytes=60 * 1024 * 1024)


def dot(a, b, ca=1, cb=0):
    return lax.dot_general(a, b, (((ca,), (cb,)), ((), ())), preferred_element_type=F32)


def call(kernel, outs, specs, *args):
    return pl.pallas_call(
        kernel,
        out_shape=outs,
        in_specs=specs,
        out_specs=jax.tree.map(lambda _: VM, outs),
        compiler_params=PARAMS,
    )(*args)


def arr(shape, dtype):
    return jax.ShapeDtypeStruct(shape, dtype)


def rows_at(row_of, count):
    n = row_of.shape[1]
    return jnp.where(lax.broadcasted_iota(jnp.int32, (count, n), 0) == row_of, 1.0, 0.0).astype(BF)


def slot_rows(shape, dim):
    i = lax.broadcasted_iota(jnp.int32, shape, dim)
    return ((i >> 2) & 1) * 64 + ((i >> 1) & 1) * 32 + (i >> 3) * 2 + (i & 1)


def placement(image_row):
    row = lax.broadcasted_iota(jnp.int32, (64, 64), 0)
    col = lax.broadcasted_iota(jnp.int32, (64, 64), 1)
    image_rows = jnp.broadcast_to(image_row, (64, 64))
    image_col = jnp.sum(jnp.where(row == col, image_rows, 0), axis=1, keepdims=True)
    alike = jnp.where((image_col == image_rows) & (row != col), 1.0, 0.0)
    twin_col = jnp.sum(alike, axis=1, keepdims=True)
    twin_row = jnp.sum(alike, axis=0, keepdims=True)
    rank = jnp.sum(jnp.where((row < col) & (twin_col == twin_row), 1.0, 0.0), axis=0, keepdims=True)
    twins = jnp.sum(twin_row, axis=1, keepdims=True)
    place = rank + jnp.where(twin_row > 0, 0.0, twins)
    lane = lax.broadcasted_iota(jnp.int32, (64, 512), 1)
    block = lax.broadcasted_iota(jnp.int32, (64, 512), 0)
    widen = jnp.where(((lane >> 1) & 63) == block, 1.0, 0.0).astype(BF)
    wide = dot(jnp.broadcast_to(place, (8, 64)).astype(BF), widen).astype(jnp.int32)
    lane = lax.broadcasted_iota(jnp.int32, (8, 512), 1)
    slot_r = (wide & 1) * 2 + (lane & 1) + ((lane >> 7) & 1) * 4
    dst = (wide >> 1) * 8 + slot_r
    back = (wide >> 1) * 16 + ((lane >> 8) & 1) * 8 + slot_r
    return dst, jnp.broadcast_to(twins, (8, 512)).astype(jnp.int32), back


def picked_columns():
    k = lax.broadcasted_iota(jnp.int32, (1, 640), 1)
    eights = ((k >> 3) & 15) * 40 + ((k >> 7) & 1) * 20 + (k >> 8) * 8 + (k & 7)
    fours = ((k >> 2) & 15) * 40 + ((k >> 6) & 1) * 20 + 16 + (k & 3)
    return jnp.where(k < 512, eights, fours)


def by_core(x):
    pick = rows_at(picked_columns(), 640)
    halves = [dot(x[:, :640], pick).astype(BF), dot(x[:, 640:], pick).astype(BF)]
    return [
        jnp.concatenate(
            [h[:, at + t * n:at + (t + 1) * n] for at, n in ((0, 128), (256, 128), (512, 64)) for h in halves], axis=1
        )
        for t in range(2)
    ]


def send_kernel(qkv_hbm, grad_hbm, image_hbm, out_ref, info_ref, qkv_ref, grad_ref, image_ref, sems):
    pairs = ((image_hbm, image_ref), (grad_hbm, grad_ref), (qkv_hbm, qkv_ref))
    copies = [pltpu.make_async_copy(a, b, sems.at[n]) for n, (a, b) in enumerate(pairs)]
    for copy in copies:
        copy.start()
    copies[0].wait()
    dst, twins, back = placement(image_ref[...])
    info_ref[...] = jnp.concatenate([dst, twins, back], axis=0)
    move = rows_at(dst[:1, :256], 256)
    copies[1].wait()
    grads = by_core(grad_ref[...].reshape(128, 1280))
    copies[2].wait()
    qkv = qkv_ref[...].reshape(128, 1920)
    for t in range(2):
        query, key, value = [qkv[:, g * 640 + t * 320:g * 640 + (t + 1) * 320] for g in range(3)]
        first = [grads[t][:, 512:], query, key, jnp.zeros((128, 64), BF)]
        second = [grads[t][:, :512], value]
        stack = jnp.concatenate([jnp.concatenate(first, axis=1), jnp.concatenate(second, axis=1)], axis=0)
        out_ref[:, t] = dot(move, stack).reshape(32, 8, 832).astype(BF)


def head_masks(rows):
    lane = lax.broadcasted_iota(jnp.int32, (rows, 320), 1)
    return [(lane >= h * HD) & (lane < (h + 1) * HD) for h in range(4)]


def by_head(x, masks):
    zero = jnp.zeros_like(x)
    return jnp.concatenate([jnp.where(m, x, zero) for m in masks], axis=0)


def own_head(x, masks):
    total = jnp.zeros((256, 320), F32)
    for h, m in enumerate(masks):
        total = jnp.where(m, x[h * 256:(h + 1) * 256], total)
    return total


def by_kind(got_ref):
    sel = rows_at(slot_rows((1, 128), 1), 128)
    quarters = [dot(sel, got_ref[n * 128:(n + 1) * 128, :]).astype(BF) for n in range(4)]
    first = jnp.concatenate([x[:64] for x in quarters], axis=0)
    second = jnp.concatenate([x[64:] for x in quarters], axis=0)
    grad = jnp.concatenate([second[:, :512], first[:, :128]], axis=1)
    return first[:, 128:448], first[:, 448:768], second[:, 512:], grad


def head_probs(own_ref, info_ref, query, key, masks):
    scores = dot(by_head(query, masks), key, 1, 1) * (HD ** -0.5)
    row = lax.broadcasted_iota(jnp.int32, (256, 256), 0)
    col = lax.broadcasted_iota(jnp.int32, (256, 256), 1)
    twins = info_ref[8:9, :256]
    apart = (((row ^ col) >> 5) & 1) > jnp.where(2 * own_ref[0] < twins, 1, 0)
    heads = []
    for h in range(4):
        own = jnp.where(apart, masked_score, scores[h * 256:(h + 1) * 256])
        exp_scores = jnp.exp(own - jnp.max(own, axis=-1, keepdims=True))
        heads.append(exp_scores / jnp.sum(exp_scores, axis=-1, keepdims=True))
    return jnp.concatenate(heads, axis=0)


def attend_kernel(own_ref, info_ref, got_ref, att_ref, grad_ref):
    query, key, value, grad_ref[...] = by_kind(got_ref)
    masks = head_masks(256)
    probs = head_probs(own_ref, info_ref, query, key, masks)
    att_ref[...] = own_head(dot(probs.astype(BF), value), masks).astype(BF)


def back_kernel(core_ref, own_ref, info_ref, got_ref, att_ref, other_ref, weight_ref, out_ref):
    query, key, value, grad = by_kind(got_ref)
    core = core_ref[0] == 0
    weights = by_core(jnp.where(core, weight_ref[:320, :], weight_ref[320:, :]))
    delta = dot(grad, jnp.where(core, weights[0], weights[1]), 1, 1)
    delta = (delta + dot(other_ref[...], jnp.where(core, weights[1], weights[0]), 1, 1)).astype(BF)
    masks = head_masks(256)
    query_heads, delta_heads = by_head(query, masks), by_head(delta, masks)
    probs = head_probs(own_ref, info_ref, query, key, masks)
    prob_grad = dot(delta_heads, value, 1, 1)
    centre = jnp.sum(probs * prob_grad, axis=-1, keepdims=True)
    score_grad = (probs * (prob_grad - centre) * (HD ** -0.5)).astype(BF)
    query_grad = own_head(dot(score_grad, key), masks).astype(BF)
    key_grad = dot(score_grad, query_heads, 0, 0).astype(BF)
    value_grad = dot(probs.astype(BF), delta_heads, 0, 0).astype(BF)
    first = jnp.concatenate([att_ref[...], query_grad], axis=1)
    second = jnp.concatenate([key_grad, value_grad], axis=1)
    lane = lax.broadcasted_iota(jnp.int32, (128, 128), 1)
    back = jnp.where(lane == slot_rows((128, 1), 0), 1.0, 0.0).astype(BF)
    for n in range(4):
        stack = jnp.concatenate([first[n * 64:(n + 1) * 64], second[n * 64:(n + 1) * 64]], axis=0)
        out_ref[n * 128:(n + 1) * 128, :] = dot(back, stack).astype(BF)


def weight_kernel(core_ref, grad_ref, own_ref, other_ref, out_ref):
    grad = grad_ref[...]
    first = core_ref[0] == 0
    own, other = own_ref[...], other_ref[...]
    att = jnp.concatenate([jnp.where(first, own, other), jnp.where(first, other, own)], axis=1)
    part = dot(grad, att, 0, 0)
    row = lax.broadcasted_iota(jnp.int32, (256, 128), 0)
    col = lax.broadcasted_iota(jnp.int32, (256, 128), 1)
    twice = dot(jnp.where((row >> 1) == col, 1.0, 0.0).astype(BF), part[512:].astype(BF))
    odd = (lax.broadcasted_iota(jnp.int32, (256, 320), 0) & 1) == 1
    rest = jnp.where(odd, twice[:, 320:], twice[:, :320])
    sums = dot(jnp.ones((8, 256), BF), grad)[:1]
    row = lax.broadcasted_iota(jnp.int32, (256, 640), 0)
    col = lax.broadcasted_iota(jnp.int32, (256, 640), 1)
    col_sp = jnp.where(col < 512, (col >> 3) & 31, (col >> 2) & 31)
    own_sums = jnp.where(col_sp == (row >> 3), sums, 0.0).astype(BF)
    k = lax.broadcasted_iota(jnp.int32, (640, 64), 0)
    lane = lax.broadcasted_iota(jnp.int32, (640, 64), 1)
    at = jnp.where(k < 512, (k >> 8) * 8 + (k & 7), 16 + (k & 3))
    bias = dot(own_sums, jnp.where(lane == at, 1.0, 0.0).astype(BF))
    out_ref[...] = jnp.concatenate([part[:256], part[256:512], rest, bias], axis=1).astype(BF)


def total_kernel(scale, got_ref, weight_ref, bias_ref):
    total = got_ref[0].astype(F32)
    for n in range(1, got_ref.shape[0]):
        total = total + got_ref[n].astype(F32)
    total = total * scale
    weight_ref[0:8, :] = total[:, :640]
    weight_ref[8:16, :] = total[:, 640:1280]
    for n in range(4):
        weight_ref[16 + n:17 + n, 0:320] = total[2 * n:2 * n + 1, 1280:1600]
        weight_ref[16 + n:17 + n, 320:640] = total[2 * n + 1:2 * n + 2, 1280:1600]
    bias_ref[...] = total[:1, 1600:]


def home_kernel(got_ref, info_ref, weight_ref, bias_ref, branch_ref, grad_ref):
    rows = dot(rows_at(info_ref[16:17, :], 512), got_ref[...], 0, 0).astype(BF)
    att = jnp.concatenate([rows[:128, :320], rows[256:384, :320]], axis=1)
    branch = dot(att, weight_ref[...]) + bias_ref[...].astype(F32)
    branch_ref[...] = branch.astype(BF).reshape(64, 2, 1280)
    for n, (p, m) in enumerate(((0, 1), (1, 0), (1, 1))):
        both = [rows[(t * 2 + p) * 128:(t * 2 + p + 1) * 128, m * 320:(m + 1) * 320] for t in range(2)]
        grad_ref[:, :, n * 640:(n + 1) * 640] = jnp.concatenate(both, axis=1).reshape(64, 2, 640)


def body(qkv, out_grad, block_image, proj_weight, proj_bias):
    own_sp, own_tp = lax.axis_index("sp"), lax.axis_index("tp")
    dp_count = lax.axis_size("dp")
    outgoing, info = pl.pallas_call(
        send_kernel,
        out_shape=(arr((32, 2, 8, 832), BF), arr((24, 512), jnp.int32)),
        in_specs=[HBM] * 3,
        out_specs=(VM, VM),
        scratch_shapes=[
            pltpu.VMEM((64, 2, 1920), BF),
            pltpu.VMEM((64, 2, 1280), BF),
            pltpu.VMEM((1, 64), jnp.int32),
            pltpu.SemaphoreType.DMA((3,)),
        ],
        compiler_params=WHOLE,
    )(qkv[0], out_grad[0], block_image)
    arrived = lax.all_to_all(
        outgoing.reshape(64, 8, 832), ("sp", "tp"), split_axis=0, concat_axis=0, tiled=True
    ).reshape(512, 832)
    own = own_sp.astype(jnp.int32)[None]
    attended, grads = call(
        attend_kernel,
        (arr((256, 320), BF), arr((256, 640), BF)),
        [SM, VM, VM], own, info, arrived,
    )
    other = lax.ppermute(attended, "tp", [(0, 1), (1, 0)])
    core = own_tp.astype(jnp.int32)[None]
    part = call(weight_kernel, arr((256, 1664), BF), [SM, VM, VM, VM], core, grads, attended, other)
    late_grads, part = lax.optimization_barrier((grads, part))
    other_grads = lax.ppermute(late_grads, "tp", [(0, 1), (1, 0)])
    returning = call(
        back_kernel, arr((512, 640), BF), [SM, SM] + [VM] * 5,
        core, own, info, arrived, attended, other_grads, proj_weight,
    )
    shares = lax.all_to_all(part.reshape(32, 8, 1664), "sp", split_axis=0, concat_axis=0, tiled=True)
    share = jnp.sum(shares.astype(F32), axis=0).astype(BF)
    share, returning = lax.optimization_barrier((share, returning))
    totals = lax.all_gather(share, "dp")
    total, sums = call(
        functools.partial(total_kernel, (dp_count * 8192) ** -0.5),
        (arr((20, 640), F32), arr((1, 64), F32)), [VM], totals,
    )
    returned = lax.all_to_all(
        returning.reshape(64, 8, 640), ("sp", "tp"), split_axis=0, concat_axis=0, tiled=True
    ).reshape(512, 640)
    branch, qkv_grad = call(
        home_kernel, (arr((64, 2, 1280), BF), arr((64, 2, 1920), BF)), [VM] * 4,
        returned, info, proj_weight, proj_bias.reshape(1, 1280),
    )
    return (
        branch[None],
        qkv_grad[None],
        total.T,
        sums[0, :20],
    )


def solution(mesh):
    in_specs = (
        P("dp", None, ("sp", "tp"), None),
        P("dp", None, ("sp", "tp"), None),
        P("dp", None),
        P(),
        P(),
    )
    out_specs = (
        P("dp", None, ("sp", "tp"), None),
        P("dp", None, ("sp", "tp"), None),
        P(None, ("sp", "tp")),
        P(("sp", "tp")),
    )
    return jax.shard_map(body, mesh=mesh, in_specs=in_specs, out_specs=out_specs, check_vma=False)
```

```python
import functools

import jax
import jax.numpy as jnp
from jax import lax
from jax.experimental import pallas as pl
from jax.experimental.pallas import tpu as pltpu
from jax.sharding import PartitionSpec as P

HD = 80
BF = jnp.bfloat16
F32 = jnp.float32
masked_score = -1e30

VM = pl.BlockSpec(memory_space=pltpu.VMEM)
SM = pl.BlockSpec(memory_space=pltpu.SMEM)
HBM = pl.BlockSpec(memory_space=pltpu.HBM)
PARAMS = pltpu.CompilerParams(vmem_limit_bytes=20 * 1024 * 1024)
WHOLE = pltpu.CompilerParams(vmem_limit_bytes=60 * 1024 * 1024)


def dot(a, b, ca=1, cb=0):
    return lax.dot_general(a, b, (((ca,), (cb,)), ((), ())), preferred_element_type=F32)


def call(kernel, outs, specs, *args):
    return pl.pallas_call(
        kernel,
        out_shape=outs,
        in_specs=specs,
        out_specs=jax.tree.map(lambda _: VM, outs),
        compiler_params=PARAMS,
    )(*args)


def arr(shape, dtype):
    return jax.ShapeDtypeStruct(shape, dtype)


def rows_at(row_of, count):
    n = row_of.shape[1]
    return jnp.where(lax.broadcasted_iota(jnp.int32, (count, n), 0) == row_of, 1.0, 0.0).astype(BF)


def slot_rows(shape, dim):
    i = lax.broadcasted_iota(jnp.int32, shape, dim)
    return ((i >> 2) & 1) * 64 + ((i >> 1) & 1) * 32 + (i >> 3) * 2 + (i & 1)


def placement(image_row):
    row = lax.broadcasted_iota(jnp.int32, (64, 64), 0)
    col = lax.broadcasted_iota(jnp.int32, (64, 64), 1)
    image_rows = jnp.broadcast_to(image_row, (64, 64))
    image_col = jnp.sum(jnp.where(row == col, image_rows, 0), axis=1, keepdims=True)
    alike = jnp.where((image_col == image_rows) & (row != col), 1.0, 0.0)
    twin_col = jnp.sum(alike, axis=1, keepdims=True)
    twin_row = jnp.sum(alike, axis=0, keepdims=True)
    rank = jnp.sum(jnp.where((row < col) & (twin_col == twin_row), 1.0, 0.0), axis=0, keepdims=True)
    twins = jnp.sum(twin_row, axis=1, keepdims=True)
    place = rank + jnp.where(twin_row > 0, 0.0, twins)
    lane = lax.broadcasted_iota(jnp.int32, (64, 512), 1)
    block = lax.broadcasted_iota(jnp.int32, (64, 512), 0)
    widen = jnp.where(((lane >> 1) & 63) == block, 1.0, 0.0).astype(BF)
    wide = dot(jnp.broadcast_to(place, (8, 64)).astype(BF), widen).astype(jnp.int32)
    lane = lax.broadcasted_iota(jnp.int32, (8, 512), 1)
    slot_r = (wide & 1) * 2 + (lane & 1) + ((lane >> 7) & 1) * 4
    dst = (wide >> 1) * 8 + slot_r
    back = (wide >> 1) * 16 + ((lane >> 8) & 1) * 8 + slot_r
    return dst, jnp.broadcast_to(twins, (8, 512)).astype(jnp.int32), back


def picked_columns():
    k = lax.broadcasted_iota(jnp.int32, (1, 640), 1)
    eights = ((k >> 3) & 15) * 40 + ((k >> 7) & 1) * 20 + (k >> 8) * 8 + (k & 7)
    fours = ((k >> 2) & 15) * 40 + ((k >> 6) & 1) * 20 + 16 + (k & 3)
    return jnp.where(k < 512, eights, fours)


def by_core(x):
    pick = rows_at(picked_columns(), 640)
    halves = [dot(x[:, :640], pick).astype(BF), dot(x[:, 640:], pick).astype(BF)]
    return [
        jnp.concatenate(
            [h[:, at + t * n:at + (t + 1) * n] for at, n in ((0, 128), (256, 128), (512, 64)) for h in halves], axis=1
        )
        for t in range(2)
    ]


def send_kernel(qkv_hbm, grad_hbm, image_hbm, out_ref, info_ref, qkv_ref, grad_ref, image_ref, sems):
    pairs = ((image_hbm, image_ref), (grad_hbm, grad_ref), (qkv_hbm, qkv_ref))
    copies = [pltpu.make_async_copy(a, b, sems.at[n]) for n, (a, b) in enumerate(pairs)]
    for copy in copies:
        copy.start()
    copies[0].wait()
    dst, twins, back = placement(image_ref[...])
    info_ref[...] = jnp.concatenate([dst, twins, back], axis=0)
    move = rows_at(dst[:1, :256], 256)
    copies[1].wait()
    grads = by_core(grad_ref[...].reshape(128, 1280))
    copies[2].wait()
    qkv = qkv_ref[...].reshape(128, 1920)
    for t in range(2):
        query, key, value = [qkv[:, g * 640 + t * 320:g * 640 + (t + 1) * 320] for g in range(3)]
        first = [grads[t][:, 512:], query, key, jnp.zeros((128, 64), BF)]
        second = [grads[t][:, :512], value]
        stack = jnp.concatenate([jnp.concatenate(first, axis=1), jnp.concatenate(second, axis=1)], axis=0)
        out_ref[:, t] = dot(move, stack).reshape(32, 8, 832).astype(BF)


def head_masks(rows):
    lane = lax.broadcasted_iota(jnp.int32, (rows, 320), 1)
    return [(lane >= h * HD) & (lane < (h + 1) * HD) for h in range(4)]


def by_head(x, masks):
    zero = jnp.zeros_like(x)
    return jnp.concatenate([jnp.where(m, x, zero) for m in masks], axis=0)


def own_head(x, masks):
    total = jnp.zeros((256, 320), F32)
    for h, m in enumerate(masks):
        total = jnp.where(m, x[h * 256:(h + 1) * 256], total)
    return total


def by_kind(got_ref):
    sel = rows_at(slot_rows((1, 128), 1), 128)
    quarters = [dot(sel, got_ref[n * 128:(n + 1) * 128, :]).astype(BF) for n in range(4)]
    first = jnp.concatenate([x[:64] for x in quarters], axis=0)
    second = jnp.concatenate([x[64:] for x in quarters], axis=0)
    grad = jnp.concatenate([second[:, :512], first[:, :128]], axis=1)
    return first[:, 128:448], first[:, 448:768], second[:, 512:], grad


def head_probs(own_ref, info_ref, query, key, masks):
    scores = dot(by_head(query, masks), key, 1, 1) * (HD ** -0.5)
    row = lax.broadcasted_iota(jnp.int32, (256, 256), 0)
    col = lax.broadcasted_iota(jnp.int32, (256, 256), 1)
    twins = info_ref[8:9, :256]
    apart = (((row ^ col) >> 5) & 1) > jnp.where(2 * own_ref[0] < twins, 1, 0)
    heads = []
    for h in range(4):
        own = jnp.where(apart, masked_score, scores[h * 256:(h + 1) * 256])
        exp_scores = jnp.exp(own - jnp.max(own, axis=-1, keepdims=True))
        heads.append(exp_scores * (1.0 / jnp.sum(exp_scores, axis=-1, keepdims=True)))
    return jnp.concatenate(heads, axis=0)


def attend_kernel(own_ref, info_ref, got_ref, att_ref, grad_ref):
    query, key, value, grad_ref[...] = by_kind(got_ref)
    masks = head_masks(256)
    probs = head_probs(own_ref, info_ref, query, key, masks)
    att_ref[...] = own_head(dot(probs.astype(BF), value), masks).astype(BF)


def back_kernel(core_ref, own_ref, info_ref, got_ref, att_ref, other_ref, weight_ref, out_ref):
    query, key, value, grad = by_kind(got_ref)
    core = core_ref[0] == 0
    weights = by_core(jnp.where(core, weight_ref[:320, :], weight_ref[320:, :]))
    delta = dot(grad, jnp.where(core, weights[0], weights[1]), 1, 1)
    delta = (delta + dot(other_ref[...], jnp.where(core, weights[1], weights[0]), 1, 1)).astype(BF)
    masks = head_masks(256)
    query_heads, delta_heads = by_head(query, masks), by_head(delta, masks)
    probs = head_probs(own_ref, info_ref, query, key, masks)
    prob_grad = dot(delta_heads, value, 1, 1)
    centre = jnp.sum(probs * prob_grad, axis=-1, keepdims=True)
    score_grad = (probs * (prob_grad - centre) * (HD ** -0.5)).astype(BF)
    query_grad = own_head(dot(score_grad, key), masks).astype(BF)
    key_grad = dot(score_grad, query_heads, 0, 0).astype(BF)
    value_grad = dot(probs.astype(BF), delta_heads, 0, 0).astype(BF)
    first = jnp.concatenate([att_ref[...], query_grad], axis=1)
    second = jnp.concatenate([key_grad, value_grad], axis=1)
    lane = lax.broadcasted_iota(jnp.int32, (128, 128), 1)
    back = jnp.where(lane == slot_rows((128, 1), 0), 1.0, 0.0).astype(BF)
    for n in range(4):
        stack = jnp.concatenate([first[n * 64:(n + 1) * 64], second[n * 64:(n + 1) * 64]], axis=0)
        out_ref[n * 128:(n + 1) * 128, :] = dot(back, stack).astype(BF)


def weight_kernel(core_ref, turned_ref, own_ref, bias_ref, other_ref, out_ref):
    first = core_ref[0] == 0
    own, other = own_ref[...], other_ref[...]
    att = jnp.concatenate([jnp.where(first, own, other), jnp.where(first, other, own)], axis=1)
    part = dot(turned_ref[...], att)
    odd = (lax.broadcasted_iota(jnp.int32, (256, 320), 0) & 1) == 1
    rest = jnp.where(odd, part[512:, 320:], part[512:, :320])
    out_ref[...] = jnp.concatenate([part[:256], part[256:512], rest, bias_ref[...]], axis=1).astype(BF)


def turn_kernel(grad_ref, turned_ref, bias_ref):
    grad = grad_ref[...]
    row = lax.broadcasted_iota(jnp.int32, (768, 1), 0)
    row = jnp.where(row < 512, row, 256 + (row >> 1))
    col = lax.broadcasted_iota(jnp.int32, (768, 640), 1)
    turned_ref[...] = dot(jnp.where(row == col, 1.0, 0.0).astype(BF), grad, 1, 1).astype(BF)
    sums = dot(jnp.ones((8, 256), BF), grad)[:1]
    row = lax.broadcasted_iota(jnp.int32, (256, 640), 0)
    col = lax.broadcasted_iota(jnp.int32, (256, 640), 1)
    col_sp = jnp.where(col < 512, (col >> 3) & 31, (col >> 2) & 31)
    own_sums = jnp.where(col_sp == (row >> 3), sums, 0.0).astype(BF)
    k = lax.broadcasted_iota(jnp.int32, (640, 64), 0)
    lane = lax.broadcasted_iota(jnp.int32, (640, 64), 1)
    at = jnp.where(k < 512, (k >> 8) * 8 + (k & 7), 16 + (k & 3))
    bias_ref[...] = dot(own_sums, jnp.where(lane == at, 1.0, 0.0).astype(BF))


def share_kernel(got_ref, out_ref):
    total = got_ref[0].astype(F32)
    for n in range(1, got_ref.shape[0]):
        total = total + got_ref[n].astype(F32)
    out_ref[...] = total.astype(BF)


def total_kernel(scale, got_ref, weight_ref, bias_ref):
    total = got_ref[0].astype(F32)
    for n in range(1, got_ref.shape[0]):
        total = total + got_ref[n].astype(F32)
    total = total * scale
    weight_ref[0:8, :] = total[:, :640]
    weight_ref[8:16, :] = total[:, 640:1280]
    for n in range(4):
        weight_ref[16 + n:17 + n, 0:320] = total[2 * n:2 * n + 1, 1280:1600]
        weight_ref[16 + n:17 + n, 320:640] = total[2 * n + 1:2 * n + 2, 1280:1600]
    bias_ref[...] = total[:1, 1600:1620]


def home_kernel(got_ref, info_ref, weight_ref, bias_ref, branch_ref, grad_ref):
    rows = dot(rows_at(info_ref[16:17, :], 512), got_ref[...], 0, 0).astype(BF)
    att = jnp.concatenate([rows[:128, :320], rows[256:384, :320]], axis=1)
    branch = dot(att, weight_ref[...]) + bias_ref[...].astype(F32)
    branch_ref[...] = branch.astype(BF).reshape(64, 2, 1280)
    for n, (p, m) in enumerate(((0, 1), (1, 0), (1, 1))):
        both = [rows[(t * 2 + p) * 128:(t * 2 + p + 1) * 128, m * 320:(m + 1) * 320] for t in range(2)]
        grad_ref[:, :, n * 640:(n + 1) * 640] = jnp.concatenate(both, axis=1).reshape(64, 2, 640)


def body(qkv, out_grad, block_image, proj_weight, proj_bias):
    own_sp, own_tp = lax.axis_index("sp"), lax.axis_index("tp")
    dp_count = lax.axis_size("dp")
    outgoing, info = pl.pallas_call(
        send_kernel,
        out_shape=(arr((32, 2, 8, 832), BF), arr((24, 512), jnp.int32)),
        in_specs=[HBM] * 3,
        out_specs=(VM, VM),
        scratch_shapes=[
            pltpu.VMEM((64, 2, 1920), BF),
            pltpu.VMEM((64, 2, 1280), BF),
            pltpu.VMEM((1, 64), jnp.int32),
            pltpu.SemaphoreType.DMA((3,)),
        ],
        compiler_params=WHOLE,
    )(qkv[0], out_grad[0], block_image)
    arrived = lax.all_to_all(
        outgoing.reshape(64, 8, 832), ("sp", "tp"), split_axis=0, concat_axis=0, tiled=True
    ).reshape(512, 832)
    own = own_sp.astype(jnp.int32)[None]
    attended, grads = call(
        attend_kernel,
        (arr((256, 320), BF), arr((256, 640), BF)),
        [SM, VM, VM], own, info, arrived,
    )
    other = lax.ppermute(attended, "tp", [(0, 1), (1, 0)])
    core = own_tp.astype(jnp.int32)[None]
    turned, sums = call(turn_kernel, (arr((768, 256), BF), arr((256, 64), F32)), [VM], grads)
    part = call(weight_kernel, arr((256, 1664), BF), [SM] + [VM] * 4, core, turned, attended, sums, other)
    late_grads, part = lax.optimization_barrier((grads, part))
    other_grads = lax.ppermute(late_grads, "tp", [(0, 1), (1, 0)])
    returning = call(
        back_kernel, arr((512, 640), BF), [SM, SM] + [VM] * 5,
        core, own, info, arrived, attended, other_grads, proj_weight,
    )
    shares = lax.all_to_all(part.reshape(32, 8, 1664), "sp", split_axis=0, concat_axis=0, tiled=True)
    share = jnp.sum(shares.astype(F32), axis=0).astype(BF)
    share, returning = lax.optimization_barrier((share, returning))
    totals = lax.all_gather(share, "dp")
    total, sums = call(
        functools.partial(total_kernel, (dp_count * 8192) ** -0.5),
        (arr((20, 640), F32), arr((1, 20), F32)), [VM], totals,
    )
    returned = lax.all_to_all(
        returning.reshape(64, 8, 640), ("sp", "tp"), split_axis=0, concat_axis=0, tiled=True
    ).reshape(512, 640)
    branch, qkv_grad = call(
        home_kernel, (arr((64, 2, 1280), BF), arr((64, 2, 1920), BF)), [VM] * 4,
        returned, info, proj_weight, proj_bias.reshape(1, 1280),
    )
    return (
        branch[None],
        qkv_grad[None],
        total.T,
        sums.reshape(20),
    )


def solution(mesh):
    in_specs = (
        P("dp", None, ("sp", "tp"), None),
        P("dp", None, ("sp", "tp"), None),
        P("dp", None),
        P(),
        P(),
    )
    out_specs = (
        P("dp", None, ("sp", "tp"), None),
        P("dp", None, ("sp", "tp"), None),
        P(None, ("sp", "tp")),
        P(("sp", "tp")),
    )
    return jax.shard_map(body, mesh=mesh, in_specs=in_specs, out_specs=out_specs, check_vma=False)
```

```python
import functools

import jax
import jax.numpy as jnp
from jax import lax
from jax.experimental import pallas as pl
from jax.experimental.pallas import tpu as pltpu
from jax.sharding import PartitionSpec as P

HD = 80
BF = jnp.bfloat16
F32 = jnp.float32
masked_score = -1e30

VM = pl.BlockSpec(memory_space=pltpu.VMEM)
SM = pl.BlockSpec(memory_space=pltpu.SMEM)
HBM = pl.BlockSpec(memory_space=pltpu.HBM)
PARAMS = pltpu.CompilerParams(vmem_limit_bytes=20 * 1024 * 1024)
WHOLE = pltpu.CompilerParams(vmem_limit_bytes=60 * 1024 * 1024)


def dot(a, b, ca=1, cb=0):
    return lax.dot_general(a, b, (((ca,), (cb,)), ((), ())), preferred_element_type=F32)


def call(kernel, outs, specs, *args):
    return pl.pallas_call(
        kernel,
        out_shape=outs,
        in_specs=specs,
        out_specs=jax.tree.map(lambda _: VM, outs),
        compiler_params=PARAMS,
    )(*args)


def arr(shape, dtype):
    return jax.ShapeDtypeStruct(shape, dtype)


def rows_at(row_of, count):
    n = row_of.shape[1]
    return jnp.where(lax.broadcasted_iota(jnp.int32, (count, n), 0) == row_of, 1.0, 0.0).astype(BF)


def slot_rows(shape, dim):
    i = lax.broadcasted_iota(jnp.int32, shape, dim)
    return ((i >> 2) & 1) * 64 + ((i >> 1) & 1) * 32 + (i >> 3) * 2 + (i & 1)


def placement(image_row):
    row = lax.broadcasted_iota(jnp.int32, (64, 64), 0)
    col = lax.broadcasted_iota(jnp.int32, (64, 64), 1)
    image_rows = jnp.broadcast_to(image_row, (64, 64))
    image_col = jnp.sum(jnp.where(row == col, image_rows, 0), axis=1, keepdims=True)
    alike = jnp.where((image_col == image_rows) & (row != col), 1.0, 0.0)
    twin_col = jnp.sum(alike, axis=1, keepdims=True)
    twin_row = jnp.sum(alike, axis=0, keepdims=True)
    rank = jnp.sum(jnp.where((row < col) & (twin_col == twin_row), 1.0, 0.0), axis=0, keepdims=True)
    twins = jnp.sum(twin_row, axis=1, keepdims=True)
    place = rank + jnp.where(twin_row > 0, 0.0, twins)
    lane = lax.broadcasted_iota(jnp.int32, (64, 512), 1)
    block = lax.broadcasted_iota(jnp.int32, (64, 512), 0)
    widen = jnp.where(((lane >> 1) & 63) == block, 1.0, 0.0).astype(BF)
    wide = dot(jnp.broadcast_to(place, (8, 64)).astype(BF), widen).astype(jnp.int32)
    lane = lax.broadcasted_iota(jnp.int32, (8, 512), 1)
    slot_r = (wide & 1) * 2 + (lane & 1) + ((lane >> 7) & 1) * 4
    dst = (wide >> 1) * 8 + slot_r
    back = (wide >> 1) * 16 + ((lane >> 8) & 1) * 8 + slot_r
    return dst, jnp.broadcast_to(twins, (8, 512)).astype(jnp.int32), back


def picked_columns():
    k = lax.broadcasted_iota(jnp.int32, (1, 640), 1)
    eights = ((k >> 3) & 15) * 40 + ((k >> 7) & 1) * 20 + (k >> 8) * 8 + (k & 7)
    fours = ((k >> 2) & 15) * 40 + ((k >> 6) & 1) * 20 + 16 + (k & 3)
    return jnp.where(k < 512, eights, fours)


def by_core(x):
    pick = rows_at(picked_columns(), 640)
    halves = [dot(x[:, :640], pick).astype(BF), dot(x[:, 640:], pick).astype(BF)]
    return [
        jnp.concatenate(
            [h[:, at + t * n:at + (t + 1) * n] for at, n in ((0, 128), (256, 128), (512, 64)) for h in halves], axis=1
        )
        for t in range(2)
    ]


def send_kernel(qkv_hbm, grad_hbm, image_hbm, out_ref, info_ref, qkv_ref, grad_ref, image_ref, sems):
    pairs = ((image_hbm, image_ref), (grad_hbm, grad_ref), (qkv_hbm, qkv_ref))
    copies = [pltpu.make_async_copy(a, b, sems.at[n]) for n, (a, b) in enumerate(pairs)]
    for copy in copies:
        copy.start()
    copies[0].wait()
    dst, twins, back = placement(image_ref[...])
    info_ref[...] = jnp.concatenate([dst, twins, back], axis=0)
    move = rows_at(dst[:1, :256], 256)
    copies[1].wait()
    grads = by_core(grad_ref[...].reshape(128, 1280))
    copies[2].wait()
    qkv = qkv_ref[...].reshape(128, 1920)
    for t in range(2):
        query, key, value = [qkv[:, g * 640 + t * 320:g * 640 + (t + 1) * 320] for g in range(3)]
        first = [grads[t][:, 512:], query, key, jnp.zeros((128, 64), BF)]
        second = [grads[t][:, :512], value]
        stack = jnp.concatenate([jnp.concatenate(first, axis=1), jnp.concatenate(second, axis=1)], axis=0)
        out_ref[:, t] = dot(move, stack).reshape(32, 8, 832).astype(BF)


def head_masks(rows):
    lane = lax.broadcasted_iota(jnp.int32, (rows, 320), 1)
    return [(lane >= h * HD) & (lane < (h + 1) * HD) for h in range(4)]


def by_head(x, masks):
    zero = jnp.zeros_like(x)
    return jnp.concatenate([jnp.where(m, x, zero) for m in masks], axis=0)


def own_head(x, masks):
    total = jnp.zeros((256, 320), F32)
    for h, m in enumerate(masks):
        total = jnp.where(m, x[h * 256:(h + 1) * 256], total)
    return total


def by_kind(got_ref):
    sel = rows_at(slot_rows((1, 128), 1), 128)
    quarters = [dot(sel, got_ref[n * 128:(n + 1) * 128, :]).astype(BF) for n in range(4)]
    first = jnp.concatenate([x[:64] for x in quarters], axis=0)
    second = jnp.concatenate([x[64:] for x in quarters], axis=0)
    grad = jnp.concatenate([second[:, :512], first[:, :128]], axis=1)
    return first[:, 128:448], first[:, 448:768], second[:, 512:], grad


def head_probs(own_ref, info_ref, query, key, masks):
    scores = dot(by_head(query, masks), key, 1, 1) * (HD ** -0.5)
    row = lax.broadcasted_iota(jnp.int32, (256, 256), 0)
    col = lax.broadcasted_iota(jnp.int32, (256, 256), 1)
    twins = info_ref[8:9, :256]
    apart = (((row ^ col) >> 5) & 1) > jnp.where(2 * own_ref[0] < twins, 1, 0)
    heads = []
    for h in range(4):
        own = jnp.where(apart, masked_score, scores[h * 256:(h + 1) * 256])
        exp_scores = jnp.exp(own - jnp.max(own, axis=-1, keepdims=True))
        heads.append(exp_scores * (1.0 / jnp.sum(exp_scores, axis=-1, keepdims=True)))
    return jnp.concatenate(heads, axis=0)


def attend_kernel(own_ref, info_ref, got_ref, att_ref, grad_ref):
    query, key, value, grad_ref[...] = by_kind(got_ref)
    masks = head_masks(256)
    probs = head_probs(own_ref, info_ref, query, key, masks)
    att_ref[...] = own_head(dot(probs.astype(BF), value), masks).astype(BF)


def back_kernel(core_ref, own_ref, info_ref, got_ref, att_ref, other_ref, weight_ref, out_ref):
    query, key, value, grad = by_kind(got_ref)
    core = core_ref[0] == 0
    weights = by_core(jnp.where(core, weight_ref[:320, :], weight_ref[320:, :]))
    delta = dot(grad, jnp.where(core, weights[0], weights[1]), 1, 1)
    delta = (delta + dot(other_ref[...], jnp.where(core, weights[1], weights[0]), 1, 1)).astype(BF)
    masks = head_masks(256)
    query_heads, delta_heads = by_head(query, masks), by_head(delta, masks)
    probs = head_probs(own_ref, info_ref, query, key, masks)
    prob_grad = dot(delta_heads, value, 1, 1)
    centre = jnp.sum(probs * prob_grad, axis=-1, keepdims=True)
    score_grad = (probs * (prob_grad - centre) * (HD ** -0.5)).astype(BF)
    query_grad = own_head(dot(score_grad, key), masks).astype(BF)
    key_grad = dot(score_grad, query_heads, 0, 0).astype(BF)
    value_grad = dot(probs.astype(BF), delta_heads, 0, 0).astype(BF)
    first = jnp.concatenate([att_ref[...], query_grad], axis=1)
    second = jnp.concatenate([key_grad, value_grad], axis=1)
    lane = lax.broadcasted_iota(jnp.int32, (128, 128), 1)
    back = jnp.where(lane == slot_rows((128, 1), 0), 1.0, 0.0).astype(BF)
    for n in range(4):
        stack = jnp.concatenate([first[n * 64:(n + 1) * 64], second[n * 64:(n + 1) * 64]], axis=0)
        out_ref[n * 128:(n + 1) * 128, :] = dot(back, stack).astype(BF)


def weight_kernel(core_ref, turned_ref, own_ref, bias_ref, other_ref, out_ref):
    first = core_ref[0] == 0
    own, other = own_ref[...], other_ref[...]
    att = jnp.concatenate([jnp.where(first, own, other), jnp.where(first, other, own)], axis=1)
    part = dot(turned_ref[...], att)
    odd = (lax.broadcasted_iota(jnp.int32, (256, 320), 0) & 1) == 1
    rest = jnp.where(odd, part[512:, 320:], part[512:, :320])
    out_ref[...] = jnp.concatenate([part[:256], part[256:512], rest, bias_ref[...]], axis=1).astype(BF)


def turn_kernel(grad_ref, turned_ref, bias_ref):
    grad = grad_ref[...]
    row = lax.broadcasted_iota(jnp.int32, (768, 1), 0)
    row = jnp.where(row < 512, row, 256 + (row >> 1))
    col = lax.broadcasted_iota(jnp.int32, (768, 640), 1)
    turned_ref[...] = dot(jnp.where(row == col, 1.0, 0.0).astype(BF), grad, 1, 1).astype(BF)
    sums = dot(jnp.ones((8, 256), BF), grad)[:1]
    row = lax.broadcasted_iota(jnp.int32, (256, 640), 0)
    col = lax.broadcasted_iota(jnp.int32, (256, 640), 1)
    col_sp = jnp.where(col < 512, (col >> 3) & 31, (col >> 2) & 31)
    own_sums = jnp.where(col_sp == (row >> 3), sums, 0.0).astype(BF)
    k = lax.broadcasted_iota(jnp.int32, (640, 64), 0)
    lane = lax.broadcasted_iota(jnp.int32, (640, 64), 1)
    at = jnp.where(k < 512, (k >> 8) * 8 + (k & 7), 16 + (k & 3))
    bias_ref[...] = dot(own_sums, jnp.where(lane == at, 1.0, 0.0).astype(BF))


def share_kernel(got_ref, out_ref):
    total = got_ref[0].astype(F32)
    for n in range(1, got_ref.shape[0]):
        total = total + got_ref[n].astype(F32)
    out_ref[...] = total.astype(BF)


def home_kernel(scale, share_ref, got_ref, info_ref, weight_ref, bias_ref, branch_ref, grad_ref, total_ref, sums_ref):
    total = share_ref[0].astype(F32)
    for n in range(1, share_ref.shape[0]):
        total = total + share_ref[n].astype(F32)
    total = total * scale
    total_ref[0:8, :] = total[:, :640]
    total_ref[8:16, :] = total[:, 640:1280]
    for n in range(4):
        total_ref[16 + n:17 + n, 0:320] = total[2 * n:2 * n + 1, 1280:1600]
        total_ref[16 + n:17 + n, 320:640] = total[2 * n + 1:2 * n + 2, 1280:1600]
    sums_ref[...] = total[:1, 1600:1620]
    rows = dot(rows_at(info_ref[16:17, :], 512), got_ref[...], 0, 0).astype(BF)
    att = jnp.concatenate([rows[:128, :320], rows[256:384, :320]], axis=1)
    branch = dot(att, weight_ref[...]) + bias_ref[...].astype(F32)
    branch_ref[...] = branch.astype(BF).reshape(64, 2, 1280)
    for n, (p, m) in enumerate(((0, 1), (1, 0), (1, 1))):
        both = [rows[(t * 2 + p) * 128:(t * 2 + p + 1) * 128, m * 320:(m + 1) * 320] for t in range(2)]
        grad_ref[:, :, n * 640:(n + 1) * 640] = jnp.concatenate(both, axis=1).reshape(64, 2, 640)


def body(qkv, out_grad, block_image, proj_weight, proj_bias):
    own_sp, own_tp = lax.axis_index("sp"), lax.axis_index("tp")
    dp_count = lax.axis_size("dp")
    outgoing, info = pl.pallas_call(
        send_kernel,
        out_shape=(arr((32, 2, 8, 832), BF), arr((24, 512), jnp.int32)),
        in_specs=[HBM] * 3,
        out_specs=(VM, VM),
        scratch_shapes=[
            pltpu.VMEM((64, 2, 1920), BF),
            pltpu.VMEM((64, 2, 1280), BF),
            pltpu.VMEM((1, 64), jnp.int32),
            pltpu.SemaphoreType.DMA((3,)),
        ],
        compiler_params=WHOLE,
    )(qkv[0], out_grad[0], block_image)
    arrived = lax.all_to_all(
        outgoing.reshape(64, 8, 832), ("sp", "tp"), split_axis=0, concat_axis=0, tiled=True
    ).reshape(512, 832)
    own = own_sp.astype(jnp.int32)[None]
    attended, grads = call(
        attend_kernel,
        (arr((256, 320), BF), arr((256, 640), BF)),
        [SM, VM, VM], own, info, arrived,
    )
    other = lax.ppermute(attended, "tp", [(0, 1), (1, 0)])
    core = own_tp.astype(jnp.int32)[None]
    turned, sums = call(turn_kernel, (arr((768, 256), BF), arr((256, 64), F32)), [VM], grads)
    part = call(weight_kernel, arr((256, 1664), BF), [SM] + [VM] * 4, core, turned, attended, sums, other)
    late_grads, part = lax.optimization_barrier((grads, part))
    other_grads = lax.ppermute(late_grads, "tp", [(0, 1), (1, 0)])
    returning = call(
        back_kernel, arr((512, 640), BF), [SM, SM] + [VM] * 5,
        core, own, info, arrived, attended, other_grads, proj_weight,
    )
    shares = lax.all_to_all(part.reshape(32, 8, 1664), "sp", split_axis=0, concat_axis=0, tiled=True)
    share = jnp.sum(shares.astype(F32), axis=0).astype(BF)
    share, returning = lax.optimization_barrier((share, returning))
    totals = lax.all_gather(share, "dp")
    returned = lax.all_to_all(
        returning.reshape(64, 8, 640), ("sp", "tp"), split_axis=0, concat_axis=0, tiled=True
    ).reshape(512, 640)
    branch, qkv_grad, total, sums = call(
        functools.partial(home_kernel, (dp_count * 8192) ** -0.5),
        (arr((64, 2, 1280), BF), arr((64, 2, 1920), BF), arr((20, 640), F32), arr((1, 20), F32)), [VM] * 5,
        totals, returned, info, proj_weight, proj_bias.reshape(1, 1280),
    )
    return (
        branch[None],
        qkv_grad[None],
        total.T,
        sums.reshape(20),
    )


def solution(mesh):
    in_specs = (
        P("dp", None, ("sp", "tp"), None),
        P("dp", None, ("sp", "tp"), None),
        P("dp", None),
        P(),
        P(),
    )
    out_specs = (
        P("dp", None, ("sp", "tp"), None),
        P("dp", None, ("sp", "tp"), None),
        P(None, ("sp", "tp")),
        P(("sp", "tp")),
    )
    return jax.shard_map(body, mesh=mesh, in_specs=in_specs, out_specs=out_specs, check_vma=False)
```

```python
import functools

import jax
import jax.numpy as jnp
from jax import lax
from jax.experimental import pallas as pl
from jax.experimental.pallas import tpu as pltpu
from jax.sharding import PartitionSpec as P

HD = 80
BF = jnp.bfloat16
F32 = jnp.float32
masked_score = -1e30

VM = pl.BlockSpec(memory_space=pltpu.VMEM)
SM = pl.BlockSpec(memory_space=pltpu.SMEM)
HBM = pl.BlockSpec(memory_space=pltpu.HBM)
PARAMS = pltpu.CompilerParams(vmem_limit_bytes=20 * 1024 * 1024)
WHOLE = pltpu.CompilerParams(vmem_limit_bytes=60 * 1024 * 1024)


def dot(a, b, ca=1, cb=0):
    return lax.dot_general(a, b, (((ca,), (cb,)), ((), ())), preferred_element_type=F32)


def call(kernel, outs, specs, *args):
    return pl.pallas_call(
        kernel,
        out_shape=outs,
        in_specs=specs,
        out_specs=jax.tree.map(lambda _: VM, outs),
        compiler_params=PARAMS,
    )(*args)


def arr(shape, dtype):
    return jax.ShapeDtypeStruct(shape, dtype)


def rows_at(row_of, count):
    n = row_of.shape[1]
    return jnp.where(lax.broadcasted_iota(jnp.int32, (count, n), 0) == row_of, 1.0, 0.0).astype(BF)


def slot_rows(shape, dim):
    i = lax.broadcasted_iota(jnp.int32, shape, dim)
    return ((i >> 2) & 1) * 64 + ((i >> 1) & 1) * 32 + (i >> 3) * 2 + (i & 1)


def placement(image_row):
    row = lax.broadcasted_iota(jnp.int32, (64, 64), 0)
    col = lax.broadcasted_iota(jnp.int32, (64, 64), 1)
    image_rows = jnp.broadcast_to(image_row, (64, 64))
    image_col = jnp.sum(jnp.where(row == col, image_rows, 0), axis=1, keepdims=True)
    alike = jnp.where((image_col == image_rows) & (row != col), 1.0, 0.0)
    twin_col = jnp.sum(alike, axis=1, keepdims=True)
    twin_row = jnp.sum(alike, axis=0, keepdims=True)
    rank = jnp.sum(jnp.where((row < col) & (twin_col == twin_row), 1.0, 0.0), axis=0, keepdims=True)
    twins = jnp.sum(twin_row, axis=1, keepdims=True)
    place = rank + jnp.where(twin_row > 0, 0.0, twins)
    lane = lax.broadcasted_iota(jnp.int32, (64, 512), 1)
    block = lax.broadcasted_iota(jnp.int32, (64, 512), 0)
    widen = jnp.where(((lane >> 1) & 63) == block, 1.0, 0.0).astype(BF)
    wide = dot(jnp.broadcast_to(place, (8, 64)).astype(BF), widen).astype(jnp.int32)
    lane = lax.broadcasted_iota(jnp.int32, (8, 512), 1)
    slot_r = (wide & 1) * 2 + (lane & 1) + ((lane >> 7) & 1) * 4
    dst = (wide >> 1) * 8 + slot_r
    back = (wide >> 1) * 16 + ((lane >> 8) & 1) * 8 + slot_r
    return dst, jnp.broadcast_to(twins, (8, 512)).astype(jnp.int32), back


def picked_columns():
    k = lax.broadcasted_iota(jnp.int32, (1, 640), 1)
    eights = ((k >> 3) & 15) * 40 + ((k >> 7) & 1) * 20 + (k >> 8) * 8 + (k & 7)
    fours = ((k >> 2) & 15) * 40 + ((k >> 6) & 1) * 20 + 16 + (k & 3)
    return jnp.where(k < 512, eights, fours)


def by_core(x, pick):
    halves = [dot(x[:, :640], pick).astype(BF), dot(x[:, 640:], pick).astype(BF)]
    return [
        jnp.concatenate(
            [h[:, at + t * n:at + (t + 1) * n] for at, n in ((0, 128), (256, 128), (512, 64)) for h in halves], axis=1
        )
        for t in range(2)
    ]


def send_kernel(qkv_hbm, grad_hbm, image_hbm, out_ref, info_ref, qkv_ref, grad_ref, image_ref, sems):
    pairs = ((image_hbm, image_ref), (grad_hbm, grad_ref), (qkv_hbm, qkv_ref))
    copies = [pltpu.make_async_copy(a, b, sems.at[n]) for n, (a, b) in enumerate(pairs)]
    for copy in copies:
        copy.start()
    pick = rows_at(picked_columns(), 640)
    copies[0].wait()
    dst, twins, back = placement(image_ref[...])
    info_ref[...] = jnp.concatenate([dst, twins, back], axis=0)
    move = rows_at(dst[:1, :256], 256)
    copies[1].wait()
    grads = by_core(grad_ref[...].reshape(128, 1280), pick)
    copies[2].wait()
    qkv = qkv_ref[...].reshape(128, 1920)
    for t in range(2):
        query, key, value = [qkv[:, g * 640 + t * 320:g * 640 + (t + 1) * 320] for g in range(3)]
        first = [grads[t][:, 512:], query, key, jnp.zeros((128, 64), BF)]
        second = [grads[t][:, :512], value]
        stack = jnp.concatenate([jnp.concatenate(first, axis=1), jnp.concatenate(second, axis=1)], axis=0)
        out_ref[:, t] = dot(move, stack).reshape(32, 8, 832).astype(BF)


def head_masks(rows):
    lane = lax.broadcasted_iota(jnp.int32, (rows, 320), 1)
    return [(lane >= h * HD) & (lane < (h + 1) * HD) for h in range(4)]


def by_head(x, masks):
    zero = jnp.zeros_like(x)
    return jnp.concatenate([jnp.where(m, x, zero) for m in masks], axis=0)


def own_head(x, masks):
    total = jnp.zeros((256, 320), F32)
    for h, m in enumerate(masks):
        total = jnp.where(m, x[h * 256:(h + 1) * 256], total)
    return total


def by_kind(got_ref):
    sel = rows_at(slot_rows((1, 128), 1), 128)
    quarters = [dot(sel, got_ref[n * 128:(n + 1) * 128, :]).astype(BF) for n in range(4)]
    first = jnp.concatenate([x[:64] for x in quarters], axis=0)
    second = jnp.concatenate([x[64:] for x in quarters], axis=0)
    grad = jnp.concatenate([second[:, :512], first[:, :128]], axis=1)
    return first[:, 128:448], first[:, 448:768], second[:, 512:], grad


def head_exps(own_ref, info_ref, query, key, masks):
    scores = dot(by_head(query, masks), key, 1, 1) * (HD ** -0.5)
    row = lax.broadcasted_iota(jnp.int32, (256, 256), 0)
    col = lax.broadcasted_iota(jnp.int32, (256, 256), 1)
    twins = info_ref[8:9, :256]
    apart = (((row ^ col) >> 5) & 1) > jnp.where(2 * own_ref[0] < twins, 1, 0)
    heads = []
    for h in range(4):
        own = jnp.where(apart, masked_score, scores[h * 256:(h + 1) * 256])
        heads.append(jnp.exp(own - jnp.max(own, axis=-1, keepdims=True)))
    return heads


def attend_kernel(own_ref, info_ref, got_ref, att_ref, grad_ref):
    query, key, value, grad_ref[...] = by_kind(got_ref)
    masks = head_masks(256)
    heads = head_exps(own_ref, info_ref, query, key, masks)
    summed = jnp.concatenate([value, jnp.ones((256, 64), BF)], axis=1)
    total = jnp.zeros((256, 320), F32)
    for exp_scores, mask in zip(heads, masks):
        both = dot(exp_scores.astype(BF), summed)
        total = jnp.where(mask, both[:, :320] * (1.0 / both[:, 320:321]), total)
    att_ref[...] = total.astype(BF)


def back_kernel(core_ref, own_ref, info_ref, got_ref, att_ref, other_ref, weight_ref, out_ref):
    query, key, value, grad = by_kind(got_ref)
    core = core_ref[0] == 0
    weights = by_core(jnp.where(core, weight_ref[:320, :], weight_ref[320:, :]), rows_at(picked_columns(), 640))
    delta = dot(grad, jnp.where(core, weights[0], weights[1]), 1, 1)
    delta = (delta + dot(other_ref[...], jnp.where(core, weights[1], weights[0]), 1, 1)).astype(BF)
    masks = head_masks(256)
    query_heads, delta_heads = by_head(query, masks), by_head(delta, masks)
    heads = head_exps(own_ref, info_ref, query, key, masks)
    probs = jnp.concatenate([x * (1.0 / jnp.sum(x, axis=-1, keepdims=True)) for x in heads], axis=0)
    prob_grad = dot(delta_heads, value, 1, 1)
    centre = jnp.sum(probs * prob_grad, axis=-1, keepdims=True)
    score_grad = (probs * (prob_grad - centre) * (HD ** -0.5)).astype(BF)
    query_grad = own_head(dot(score_grad, key), masks).astype(BF)
    key_grad = dot(score_grad, query_heads, 0, 0).astype(BF)
    value_grad = dot(probs.astype(BF), delta_heads, 0, 0).astype(BF)
    first = jnp.concatenate([att_ref[...], query_grad], axis=1)
    second = jnp.concatenate([key_grad, value_grad], axis=1)
    lane = lax.broadcasted_iota(jnp.int32, (128, 128), 1)
    back = jnp.where(lane == slot_rows((128, 1), 0), 1.0, 0.0).astype(BF)
    for n in range(4):
        stack = jnp.concatenate([first[n * 64:(n + 1) * 64], second[n * 64:(n + 1) * 64]], axis=0)
        out_ref[n * 128:(n + 1) * 128, :] = dot(back, stack).astype(BF)


def weight_kernel(core_ref, turned_ref, own_ref, bias_ref, other_ref, out_ref):
    first = core_ref[0] == 0
    own, other = own_ref[...], other_ref[...]
    att = jnp.concatenate([jnp.where(first, own, other), jnp.where(first, other, own)], axis=1)
    part = dot(turned_ref[...], att)
    odd = (lax.broadcasted_iota(jnp.int32, (256, 320), 0) & 1) == 1
    rest = jnp.where(odd, part[512:, 320:], part[512:, :320])
    out_ref[...] = jnp.concatenate([part[:256], part[256:512], rest, bias_ref[...]], axis=1).astype(BF)


def turn_kernel(grad_ref, turned_ref, bias_ref):
    grad = grad_ref[...]
    row = lax.broadcasted_iota(jnp.int32, (768, 1), 0)
    row = jnp.where(row < 512, row, 256 + (row >> 1))
    col = lax.broadcasted_iota(jnp.int32, (768, 640), 1)
    turned_ref[...] = dot(jnp.where(row == col, 1.0, 0.0).astype(BF), grad, 1, 1).astype(BF)
    sums = dot(jnp.ones((8, 256), BF), grad)[:1]
    row = lax.broadcasted_iota(jnp.int32, (256, 640), 0)
    col = lax.broadcasted_iota(jnp.int32, (256, 640), 1)
    col_sp = jnp.where(col < 512, (col >> 3) & 31, (col >> 2) & 31)
    own_sums = jnp.where(col_sp == (row >> 3), sums, 0.0).astype(BF)
    k = lax.broadcasted_iota(jnp.int32, (640, 64), 0)
    lane = lax.broadcasted_iota(jnp.int32, (640, 64), 1)
    at = jnp.where(k < 512, (k >> 8) * 8 + (k & 7), 16 + (k & 3))
    bias_ref[...] = dot(own_sums, jnp.where(lane == at, 1.0, 0.0).astype(BF))


def share_kernel(got_ref, out_ref):
    total = got_ref[0].astype(F32)
    for n in range(1, got_ref.shape[0]):
        total = total + got_ref[n].astype(F32)
    out_ref[...] = total.astype(BF)


def home_kernel(scale, share_ref, got_ref, info_ref, weight_ref, bias_ref, branch_ref, grad_ref, total_ref, sums_ref):
    total = share_ref[0].astype(F32)
    for n in range(1, share_ref.shape[0]):
        total = total + share_ref[n].astype(F32)
    total = total * scale
    total_ref[0:8, :] = total[:, :640]
    total_ref[8:16, :] = total[:, 640:1280]
    for n in range(4):
        total_ref[16 + n:17 + n, 0:320] = total[2 * n:2 * n + 1, 1280:1600]
        total_ref[16 + n:17 + n, 320:640] = total[2 * n + 1:2 * n + 2, 1280:1600]
    sums_ref[...] = total[:1, 1600:1620]
    rows = dot(rows_at(info_ref[16:17, :], 512), got_ref[...], 0, 0).astype(BF)
    att = jnp.concatenate([rows[:128, :320], rows[256:384, :320]], axis=1)
    branch = dot(att, weight_ref[...]) + bias_ref[...].astype(F32)
    branch_ref[...] = branch.astype(BF).reshape(64, 2, 1280)
    for n, (p, m) in enumerate(((0, 1), (1, 0), (1, 1))):
        both = [rows[(t * 2 + p) * 128:(t * 2 + p + 1) * 128, m * 320:(m + 1) * 320] for t in range(2)]
        grad_ref[:, :, n * 640:(n + 1) * 640] = jnp.concatenate(both, axis=1).reshape(64, 2, 640)


def body(qkv, out_grad, block_image, proj_weight, proj_bias):
    own_sp, own_tp = lax.axis_index("sp"), lax.axis_index("tp")
    dp_count = lax.axis_size("dp")
    outgoing, info = pl.pallas_call(
        send_kernel,
        out_shape=(arr((32, 2, 8, 832), BF), arr((24, 512), jnp.int32)),
        in_specs=[HBM] * 3,
        out_specs=(VM, VM),
        scratch_shapes=[
            pltpu.VMEM((64, 2, 1920), BF),
            pltpu.VMEM((64, 2, 1280), BF),
            pltpu.VMEM((1, 64), jnp.int32),
            pltpu.SemaphoreType.DMA((3,)),
        ],
        compiler_params=WHOLE,
    )(qkv[0], out_grad[0], block_image)
    arrived = lax.all_to_all(
        outgoing.reshape(64, 8, 832), ("sp", "tp"), split_axis=0, concat_axis=0, tiled=True
    ).reshape(512, 832)
    own = own_sp.astype(jnp.int32)[None]
    attended, grads = call(
        attend_kernel,
        (arr((256, 320), BF), arr((256, 640), BF)),
        [SM, VM, VM], own, info, arrived,
    )
    other = lax.ppermute(attended, "tp", [(0, 1), (1, 0)])
    core = own_tp.astype(jnp.int32)[None]
    turned, sums = call(turn_kernel, (arr((768, 256), BF), arr((256, 64), F32)), [VM], grads)
    part = call(weight_kernel, arr((256, 1664), BF), [SM] + [VM] * 4, core, turned, attended, sums, other)
    late_grads, part = lax.optimization_barrier((grads, part))
    other_grads = lax.ppermute(late_grads, "tp", [(0, 1), (1, 0)])
    returning = call(
        back_kernel, arr((512, 640), BF), [SM, SM] + [VM] * 5,
        core, own, info, arrived, attended, other_grads, proj_weight,
    )
    shares = lax.all_to_all(part.reshape(32, 8, 1664), "sp", split_axis=0, concat_axis=0, tiled=True)
    share = jnp.sum(shares.astype(F32), axis=0).astype(BF)
    share, returning = lax.optimization_barrier((share, returning))
    totals = lax.all_gather(share, "dp")
    returned = lax.all_to_all(
        returning.reshape(64, 8, 640), ("sp", "tp"), split_axis=0, concat_axis=0, tiled=True
    ).reshape(512, 640)
    branch, qkv_grad, total, sums = call(
        functools.partial(home_kernel, (dp_count * 8192) ** -0.5),
        (arr((64, 2, 1280), BF), arr((64, 2, 1920), BF), arr((20, 640), F32), arr((1, 20), F32)), [VM] * 5,
        totals, returned, info, proj_weight, proj_bias.reshape(1, 1280),
    )
    return (
        branch[None],
        qkv_grad[None],
        total.T,
        sums.reshape(20),
    )


def solution(mesh):
    in_specs = (
        P("dp", None, ("sp", "tp"), None),
        P("dp", None, ("sp", "tp"), None),
        P("dp", None),
        P(),
        P(),
    )
    out_specs = (
        P("dp", None, ("sp", "tp"), None),
        P("dp", None, ("sp", "tp"), None),
        P(None, ("sp", "tp")),
        P(("sp", "tp")),
    )
    return jax.shard_map(body, mesh=mesh, in_specs=in_specs, out_specs=out_specs, check_vma=False)
```
